32 devices in a mesh: group: 4 (over y, x), fsdp: 8 (over z, core).
Axes of the slice: x: 2, y: 2, z: 4, core: 2. Of those that a mesh axis runs over, the one named last changes fastest.
Arguments:
- activations: bfloat16 [4, 2048, 8192], P('group', 'fsdp'), may hold values from -6 to 6
- cotangent: bfloat16 [4, 2048, 512], P('group', 'fsdp'), may hold values from -0.25 to 0.25
- inner_weights: float32 [4, 8192, 512], P('group', 'fsdp'), may hold values from -6 to 6
- first_moment: float32 [4, 8192, 512], P('group', 'fsdp'), may hold values from -6 to 6
- second_moment: float32 [4, 8192, 512], P('group', 'fsdp'), may hold values from 0.5 to 4
- anchor: float32 [8192, 512], P('fsdp'), may hold values from -6 to 6
- outer_momentum: float32 [8192, 512], P('fsdp'), may hold values from -6 to 6
- fragment: int32 [1], replicated, may hold values from 0 to 3
Outputs:
- input_grad: bfloat16 [4, 2048, 8192], P('group', 'fsdp')
- new_inner: float32 [4, 8192, 512], P('group', 'fsdp')
- new_first: float32 [4, 8192, 512], P('group', 'fsdp')
- new_second: float32 [4, 8192, 512], P('group', 'fsdp')
- new_anchor: float32 [8192, 512], P('fsdp')
- new_momentum: float32 [8192, 512], P('fsdp')
The draws below stay inside these ranges and needn't reach their ends.
All inputs are finite; a program needn't handle non-finite values.
Results may differ from the reference program's by a relative error of at most 0.006.
Values may be sent and summed in bfloat16 or wider, within the bound.
No kernel may reach another device: no remote copies, remote signals or barrier semaphores. Data moves between devices by JAX's collectives and lax.ppermute only.
A program may use at most 128 MiB of HBM per device.

```python
import math
import jax
import jax.numpy as jnp
from jax import lax

D = 8192
HV = 512
HEAD = 128
STEP = 100
GROUPS = 4
TOKENS = 2048
FRAGS = 4


def spiked(drawn, stream_key, source, target, blocks, factor):
    owner, partner = [(jnp.arange(drawn.shape[axis_at]) // (drawn.shape[axis_at] // blocks)).reshape([-1 if axis == axis_at else 1 for axis in range(drawn.ndim)]) for axis_at in (source, target)]
    chosen = jax.random.permutation(stream_key, blocks)[partner]
    strong = (owner == chosen) | (owner == (partner + blocks // 2) % blocks)
    return jnp.where(strong, factor * drawn, drawn)


def steps_of(own_key, dims, cuts, low, top_value):
    factor_of, own = 1.0, jax.random.fold_in(own_key, 6)
    for position, parts in cuts:
        heights = jnp.exp(jax.random.uniform(jax.random.fold_in(own, position), (parts,), jnp.float32, low / len(cuts), top_value / len(cuts)))
        factor_of = factor_of * jnp.repeat(heights, dims[position] // parts).reshape([-1 if axis == position else 1 for axis in range(len(dims))])
    return factor_of


def noise(own_key, extent, deviation, most, split=(), held_as=jnp.bfloat16):
    loudness = steps_of(own_key, extent, split, -0.22, 0.18) if split else 1.0
    entries = jax.random.normal(own_key, extent, jnp.float32) * deviation * loudness
    return jnp.minimum(jnp.maximum(entries, -most), most).astype(held_as)


def gaussian_with(rng, extent, width, most, split, heavy, held_as=jnp.bfloat16):
    result = width * jax.random.normal(rng, extent, jnp.float32)
    if split:
        result = result * steps_of(rng, extent, split, -0.22, 0.18)
    return jnp.clip(spiked(result, jax.random.fold_in(rng, 3), *heavy), -most, most).astype(held_as)


def setup_inputs(seed: int = 0) -> dict:
    streams_of = jax.random.split(jax.random.key(seed), 9)
    return {
        "activations": gaussian_with(streams_of[0], (GROUPS, TOKENS, D), 1.0, 6.0, ((0, 4), (1, 8)), (1, 2, 8, 2.0)),
        "cotangent": noise(streams_of[1], (GROUPS, TOKENS, HV), HV ** -0.5, 0.25, ((0, 4), (1, 8))),
        "inner_weights": noise(streams_of[2], (GROUPS, D, HV), 1.0, 6.0, ((0, 4), (1, 8)), jnp.float32),
        "first_moment": noise(streams_of[3], (GROUPS, D, HV), 1.0, 6.0, ((0, 4), (1, 8)), jnp.float32),
        "second_moment": jnp.clip(jnp.exp(math.log(4.0) - 2.0794415 * jax.random.uniform(streams_of[4], (GROUPS, D, HV), jnp.float32) ** steps_of(streams_of[4], (GROUPS, D, HV), ((0, 4), (1, 8)), -0.2, 0.2)), 0.5, 4.0),
        "anchor": noise(streams_of[5], (D, HV), 1.0, 6.0, ((0, 8),), jnp.float32),
        "outer_momentum": noise(streams_of[6], (D, HV), 1.0, 6.0, ((0, 8),), jnp.float32),
        "fragment": jax.random.randint(streams_of[7], (1,), 0, FRAGS).astype(jnp.int32),
    }


def reference(activations, cotangent, inner_weights, first_moment, second_moment, anchor, outer_momentum, fragment):
    low_weights = inner_weights.astype(jnp.bfloat16)

    def one_group(index):
        upstream = cotangent[index]
        input_part = lax.dot_general(upstream, low_weights[index], (((1,), (1,)), ((), ())), preferred_element_type=jnp.float32).astype(jnp.bfloat16)
        gradient = lax.dot_general(activations[index], upstream, (((0,), (0,)), ((), ())), preferred_element_type=jnp.float32)
        return (input_part, gradient)
    input_grad, gradient = lax.map(one_group, jnp.arange(GROUPS, dtype=jnp.int32))
    new_first = 0.9 * first_moment + 0.1 * gradient
    new_second = 0.95 * second_moment + 0.05 * gradient * gradient
    corr_one = 1.0 - 0.9 ** STEP
    corr_two = 1.0 - 0.95 ** STEP
    update = new_first / corr_one / (jnp.sqrt(new_second / corr_two) + 1e-08) + 0.1 * inner_weights
    stepped = inner_weights - 0.1 * update
    offset = (fragment[0] * HEAD).astype(jnp.int32)
    local_cols = lax.dynamic_slice_in_dim(stepped, offset, HEAD, 2)
    anchor_cols = lax.dynamic_slice_in_dim(anchor, offset, HEAD, 1)
    moment_cols = lax.dynamic_slice_in_dim(outer_momentum, offset, HEAD, 1)
    average = lax.optimization_barrier(jnp.sum(anchor_cols[None] - local_cols, axis=0)) / GROUPS
    moment_new = 0.9 * moment_cols + average
    anchor_next = anchor_cols - 0.7 * (average + 0.9 * moment_new)
    new_momentum = lax.dynamic_update_slice_in_dim(outer_momentum, moment_new, offset, 1)
    new_anchor = lax.dynamic_update_slice_in_dim(anchor, anchor_next, offset, 1)
    spread_cols = jnp.broadcast_to(anchor_next[None], local_cols.shape)
    new_inner = lax.dynamic_update_slice_in_dim(stepped, spread_cols, offset, 2)
    return (input_grad, new_inner, new_first, new_second, new_anchor, new_momentum)
```

```python
import functools

import jax
import jax.numpy as jnp
from jax import lax
from jax.experimental import pallas as pl
from jax.experimental.pallas import tpu as pltpu
from jax.sharding import PartitionSpec as P

HEAD = 128
STEP = 100
CORR_ONE = 1.0 - 0.9**STEP
CORR_TWO = 1.0 - 0.95**STEP
PARTS = 2
TILE = 256
BF16 = jnp.bfloat16
F32 = jnp.float32


def plain(
    activations,
    cotangent,
    inner_weights,
    first_moment,
    second_moment,
    anchor,
    outer_momentum,
    fragment,
):
    tokens_in = activations[0]
    upstream = cotangent[0]
    weights = inner_weights[0]
    low_weights = weights.astype(BF16)
    input_grad = lax.dot_general(
        upstream,
        lax.all_gather(low_weights, "fsdp", axis=0, tiled=True),
        (((1,), (1,)), ((), ())),
        preferred_element_type=F32,
    ).astype(BF16)
    gradient = lax.psum_scatter(
        lax.dot_general(tokens_in, upstream, (((0,), (0,)), ((), ())), preferred_element_type=F32),
        "fsdp",
        scatter_dimension=0,
        tiled=True,
    )
    new_first = 0.9 * first_moment[0] + 0.1 * gradient
    new_second = 0.95 * second_moment[0] + 0.05 * gradient * gradient
    update = new_first / CORR_ONE / (jnp.sqrt(new_second / CORR_TWO) + 1e-08) + 0.1 * weights
    stepped = weights - 0.1 * update
    offset = fragment[0] * HEAD
    local_cols = lax.dynamic_slice_in_dim(stepped, offset, HEAD, 1)
    anchor_cols = lax.dynamic_slice_in_dim(anchor, offset, HEAD, 1)
    moment_cols = lax.dynamic_slice_in_dim(outer_momentum, offset, HEAD, 1)
    summed = lax.psum((anchor_cols - local_cols).astype(BF16), "group").astype(F32)
    average = summed / lax.axis_size("group")
    moment_new = 0.9 * moment_cols + average
    anchor_next = anchor_cols - 0.7 * (average + 0.9 * moment_new)
    new_momentum = lax.dynamic_update_slice_in_dim(outer_momentum, moment_new, offset, 1)
    new_anchor = lax.dynamic_update_slice_in_dim(anchor, anchor_next, offset, 1)
    new_inner = lax.dynamic_update_slice_in_dim(stepped, anchor_next, offset, 1)
    return (
        input_grad[None],
        new_inner[None],
        new_first[None],
        new_second[None],
        new_anchor,
        new_momentum,
    )


def rows_by_columns(act, cot):
    return lax.dot_general(act, cot, (((0,), (0,)), ((), ())), preferred_element_type=F32)


def call(body, scalars, grid, ins, outs, aliases=None, cost=(0, 0)):
    def spec(block, where):
        if block is None:
            return pl.BlockSpec(memory_space=pl.ANY)
        return pl.BlockSpec(block, where)

    return pl.pallas_call(
        body,
        grid_spec=pltpu.PrefetchScalarGridSpec(
            num_scalar_prefetch=1,
            grid=grid,
            in_specs=[spec(b, w) for _, b, w in ins],
            out_specs=[spec(b, w) for _, _, b, w in outs],
        ),
        out_shape=[jax.ShapeDtypeStruct(s, t) for s, t, _, _ in outs],
        input_output_aliases={1 + k: v for k, v in (aliases or {}).items()},
        cost_estimate=pl.CostEstimate(flops=cost[0], bytes_accessed=cost[1], transcendentals=0),
        compiler_params=pltpu.CompilerParams(vmem_limit_bytes=40 * 1024 * 1024),
    )(scalars, *[a for a, _, _ in ins])


def hop_body(s, up_act, up_sib, down_act, down_sib, cot, cot_sib, up_in, down_in, up_out, down_out):
    for k, (act, sib, src, dst) in enumerate(
        ((up_act, up_sib, up_in, up_out), (down_act, down_sib, down_in, down_out))
    ):

        @pl.when(s[2 * k] == 1)
        def _():
            dst[...] = src[...]

        @pl.when(s[2 * k] == 0)
        def _():
            part = rows_by_columns(act[...], cot[...]) + rows_by_columns(sib[...], cot_sib[...])
            dst[...] = (src[...].astype(F32) + part).astype(BF16)


def grad_body(s, cot, *refs):
    parts = (len(refs) - 1) // 2
    out = refs[-1]
    width = cot.shape[1] // parts
    for core in range(2):

        @pl.when(pl.program_id(0) == core)
        def _():
            total = None
            for j, block in enumerate(refs[core * parts : (core + 1) * parts]):
                term = lax.dot_general(
                    cot[:, j * width : (j + 1) * width],
                    block[...],
                    (((1,), (1,)), ((), ())),
                    preferred_element_type=F32,
                )
                total = term if total is None else total + term
            out[...] = total.astype(BF16)


def adam_body(first_part, s, act, sib, cot, cot_sib, up_in, down_in, w, m, v, anchor, *rest):
    outs = rest if first_part else rest[3:]
    inner, new_m, new_v = outs[:3]
    gradient = (
        rows_by_columns(act[...], cot[...])
        + rows_by_columns(sib[...], cot_sib[...])
        + up_in[...].astype(F32)
        + down_in[...].astype(F32)
    )
    first = 0.9 * m[...] + 0.1 * gradient
    second = 0.95 * v[...] + 0.05 * gradient * gradient
    update = first / CORR_ONE / (jnp.sqrt(second / CORR_TWO) + 1e-08) + 0.1 * w[...]
    stepped = w[...] - 0.1 * update
    new_m[...] = first
    new_v[...] = second
    inner[...] = stepped
    if first_part:
        for k in range(stepped.shape[1] // HEAD):

            @pl.when(s[2] == k)
            def _():
                diff = anchor[...] - stepped[:, k * HEAD : (k + 1) * HEAD]
                outs[3][...] = diff.astype(BF16)


def outer_body(s, own, one, two, three, anchor, moment, *rest):
    inner, new_anchor, new_moment = rest[3:]
    total = (own[...].astype(F32) + one[...].astype(F32)) + (
        two[...].astype(F32) + three[...].astype(F32)
    )
    average = total / 4.0
    momentum = 0.9 * moment[...] + average
    moved = anchor[...] - 0.7 * (average + 0.9 * momentum)
    new_moment[...] = momentum
    new_anchor[...] = moved
    inner[...] = moved


def line(
    activations,
    cotangent,
    inner_weights,
    first_moment,
    second_moment,
    anchor,
    outer_momentum,
    fragment,
):
    act, cot, weights = activations[0], cotangent[0], inner_weights[0]
    moment, second = first_moment[0], second_moment[0]
    tokens, width = act.shape
    rows, columns = weights.shape
    chips = lax.axis_size("fsdp") // 2
    part = columns // PARTS
    tiles = rows // TILE
    me = lax.axis_index("fsdp")
    z, core = me // 2, me % 2
    head = fragment[0]
    chunk_of = [(head * HEAD // part + j) % PARTS for j in range(PARTS)]

    up = [(i, i + 2) for i in range(2 * chips - 2)]
    down = [(i + 2, i) for i in range(2 * chips - 2)]
    swap = [(i, i ^ 1) for i in range(2 * chips)]

    def scalars(*values):
        return jnp.stack([jnp.asarray(v, jnp.int32) for v in values])

    low = [weights[:, j * part : (j + 1) * part].astype(BF16) for j in range(PARTS)]
    ups = [[lax.ppermute(x, "fsdp", up) for x in low]]
    downs = [[lax.ppermute(x, "fsdp", down) for x in low]]
    cot_sib = lax.ppermute(cot, "fsdp", swap)
    act_sib = lax.ppermute(act, "fsdp", swap)

    def act_spec(at):
        return (tokens, TILE), lambda i, s: (0, s[at] * tiles + i)

    def cot_spec(at):
        return (tokens, part), lambda i, s: (0, s[at])

    def whole_spec():
        return (TILE, part), lambda i, s: (i, 0)

    def hop(step, j):
        zd = chips - 1 - z
        d_up = jnp.clip(chips - step + z, 0, chips - 1)
        d_down = jnp.clip(step - 1 - zd, 0, chips - 1)
        s = scalars(step <= z, 2 * d_up + core, step <= zd, 2 * d_down + core, chunk_of[j])
        return call(
            hop_body,
            s,
            (tiles,),
            [
                (act, *act_spec(1)),
                (act_sib, *act_spec(1)),
                (act, *act_spec(3)),
                (act_sib, *act_spec(3)),
                (cot, *cot_spec(4)),
                (cot_sib, *cot_spec(4)),
                (ups[step - 1][j], *whole_spec()),
                (downs[step - 1][j], *whole_spec()),
            ],
            [((rows, part), BF16, *whole_spec())] * 2,
            cost=(8 * tokens * rows * part, 2 * (4 * rows * part + 4 * rows * tokens)),
        )

    def grad(buffer, blocks, block_at):
        others = [lax.ppermute(x, "fsdp", swap) for x in blocks]
        s = scalars(2 * block_at + core, 2 * block_at + 1 - core)
        ins = [(cot, (tokens, columns), lambda i, s: (0, 0))]
        ins += [(x, (rows, part), lambda i, s: (0, 0)) for x in [*blocks, *others]]
        body = grad_body
        aliases = {}
        if buffer is not None:
            aliases = {len(ins): 0}
            ins += [(buffer, None, None)]

            def body(*refs):
                grad_body(*refs[:-2], refs[-1])

        return call(
            body,
            s,
            (2,),
            ins,
            [((tokens, width), BF16, (tokens, rows), lambda i, s: (0, s[i]))],
            aliases,
            cost=(4 * tokens * rows * columns, 4 * rows * columns + 4 * tokens * rows),
        )[0]

    for step in range(1, chips):
        sent = [hop(step, j) for j in range(PARTS)]
        ups.append([lax.ppermute(x[0], "fsdp", up) for x in sent])
        downs.append([lax.ppermute(x[1], "fsdp", down) for x in sent])

    def pick(flag, a, b):
        return [jnp.where(flag, x, y) for x, y in zip(a, b)]

    last = chips - 1
    grads = grad(None, pick(z > 0, ups[0], low), jnp.maximum(z - 1, 0))
    grads = grad(grads, pick(z < last, downs[0], low), jnp.minimum(z + 1, last))
    grads = grad(grads, pick(z < 2, downs[1], ups[1]), (z + 2) % chips)
    grads = grad(
        grads,
        pick(z == 0, downs[2], pick(z == last, ups[2], low)),
        jnp.where(z == 0, last, jnp.where(z == last, 0, z)),
    )

    def own_spec(at):
        return (TILE, part), lambda i, s: (i, s[at])

    def head_spec(at):
        return (TILE, HEAD), lambda i, s: (i, s[at])

    state = None
    for j in range(PARTS):
        s = scalars(me, chunk_of[j], head % (part // HEAD), head)
        ins = [
            (act, *act_spec(0)),
            (act_sib, *act_spec(0)),
            (cot, *cot_spec(1)),
            (cot_sib, *cot_spec(1)),
            (ups[last][j], *whole_spec()),
            (downs[last][j], *whole_spec()),
            (weights, *own_spec(1)),
            (moment, *own_spec(1)),
            (second, *own_spec(1)),
            (anchor, *head_spec(3)),
        ]
        outs = [((rows, columns), F32, *own_spec(1))] * 3
        aliases = {}
        if j == 0:
            outs += [((rows, HEAD), BF16, (TILE, HEAD), lambda i, s: (i, 0))]
        else:
            aliases = {len(ins) + k: k for k in range(3)}
            ins += [(x, None, None) for x in state]
        result = call(
            functools.partial(adam_body, j == 0),
            s,
            (tiles,),
            ins,
            outs,
            aliases,
            cost=(4 * tokens * rows * part, 28 * rows * part + 4 * rows * tokens),
        )
        state = result[:3]
        if j == 0:
            diff = result[3]
            others = [
                lax.ppermute(diff, "group", [(i, i ^ k) for i in range(4)]) for k in (1, 2, 3)
            ]
    diff_spec = ((TILE, HEAD), lambda i, s: (i, 0))
    inner, new_anchor, new_momentum = call(
        outer_body,
        scalars(head),
        (tiles,),
        [(x, *diff_spec) for x in [diff, *others]]
        + [(anchor, *head_spec(0)), (outer_momentum, *head_spec(0))]
        + [(x, None, None) for x in (state[0], anchor, outer_momentum)],
        [((rows, columns), F32, *head_spec(0))] * 3,
        {6: 0, 7: 1, 8: 2},
        cost=(0, 32 * rows * HEAD),
    )
    return grads[None], inner[None], state[1][None], state[2][None], new_anchor, new_momentum


def solution(mesh):
    in_specs = (
        P("group", "fsdp", None),
        P("group", "fsdp", None),
        P("group", "fsdp", None),
        P("group", "fsdp", None),
        P("group", "fsdp", None),
        P("fsdp", None),
        P("fsdp", None),
        P(),
    )
    out_specs = (
        P("group", "fsdp", None),
        P("group", "fsdp", None),
        P("group", "fsdp", None),
        P("group", "fsdp", None),
        P("fsdp", None),
        P("fsdp", None),
    )
    short = mesh.shape["fsdp"] == 8 and mesh.shape["group"] == 4
    return jax.shard_map(
        line if short else plain,
        mesh=mesh,
        in_specs=in_specs,
        out_specs=out_specs,
        check_vma=False,
    )
```

```python
import functools

import jax
import jax.numpy as jnp
from jax import lax
from jax.experimental import pallas as pl
from jax.experimental.pallas import tpu as pltpu
from jax.sharding import PartitionSpec as P

HEAD = 128
STEP = 100
CORR_ONE = 1.0 - 0.9**STEP
CORR_TWO = 1.0 - 0.95**STEP
PARTS = ((0, 256), (256, 256))
TILE = 256
BF16 = jnp.bfloat16
F32 = jnp.float32


def plain(
    activations,
    cotangent,
    inner_weights,
    first_moment,
    second_moment,
    anchor,
    outer_momentum,
    fragment,
):
    tokens_in = activations[0]
    upstream = cotangent[0]
    weights = inner_weights[0]
    low_weights = weights.astype(BF16)
    input_grad = lax.dot_general(
        upstream,
        lax.all_gather(low_weights, "fsdp", axis=0, tiled=True),
        (((1,), (1,)), ((), ())),
        preferred_element_type=F32,
    ).astype(BF16)
    gradient = lax.psum_scatter(
        lax.dot_general(tokens_in, upstream, (((0,), (0,)), ((), ())), preferred_element_type=F32),
        "fsdp",
        scatter_dimension=0,
        tiled=True,
    )
    new_first = 0.9 * first_moment[0] + 0.1 * gradient
    new_second = 0.95 * second_moment[0] + 0.05 * gradient * gradient
    update = new_first / CORR_ONE / (jnp.sqrt(new_second / CORR_TWO) + 1e-08) + 0.1 * weights
    stepped = weights - 0.1 * update
    offset = fragment[0] * HEAD
    local_cols = lax.dynamic_slice_in_dim(stepped, offset, HEAD, 1)
    anchor_cols = lax.dynamic_slice_in_dim(anchor, offset, HEAD, 1)
    moment_cols = lax.dynamic_slice_in_dim(outer_momentum, offset, HEAD, 1)
    summed = lax.psum((anchor_cols - local_cols).astype(BF16), "group").astype(F32)
    average = summed / lax.axis_size("group")
    moment_new = 0.9 * moment_cols + average
    anchor_next = anchor_cols - 0.7 * (average + 0.9 * moment_new)
    new_momentum = lax.dynamic_update_slice_in_dim(outer_momentum, moment_new, offset, 1)
    new_anchor = lax.dynamic_update_slice_in_dim(anchor, anchor_next, offset, 1)
    new_inner = lax.dynamic_update_slice_in_dim(stepped, anchor_next, offset, 1)
    return (
        input_grad[None],
        new_inner[None],
        new_first[None],
        new_second[None],
        new_anchor,
        new_momentum,
    )


def rows_by_columns(act, cot):
    return lax.dot_general(act, cot, (((0,), (0,)), ((), ())), preferred_element_type=F32)


def vmem(*shape, dtype=F32):
    return pltpu.VMEM(shape, dtype)


def hbm(*shape, dtype=F32):
    return jax.ShapeDtypeStruct(shape, dtype)


class Held:
    def __init__(self, array):
        self.array = array


def call(body, scalars, ins, outs, scratch=(), aliases=None, after=(), us=1.0):
    arrays, specs = [scalars], [pl.BlockSpec(memory_space=pltpu.SMEM)]
    for x in ins:
        if isinstance(x, Held):
            arrays.append(pltpu.with_memory_space_constraint(x.array, pltpu.VMEM))
            specs.append(pl.BlockSpec(memory_space=pltpu.VMEM))
        else:
            arrays.append(pltpu.with_memory_space_constraint(x, pltpu.HBM))
            specs.append(pl.BlockSpec(memory_space=pltpu.HBM))
    first = len(arrays)
    arrays += [pltpu.with_memory_space_constraint(x, pltpu.VMEM) for x in after]
    specs += [pl.BlockSpec(memory_space=pltpu.VMEM)] * len(after)

    def inner(*refs):
        body(*refs[:first], *refs[first + len(after) :])

    return pl.pallas_call(
        inner,
        in_specs=specs,
        out_specs=[
            pl.BlockSpec(memory_space=pl.ANY if isinstance(o, jax.ShapeDtypeStruct) else pltpu.VMEM)
            for o in outs
        ],
        out_shape=list(outs),
        scratch_shapes=list(scratch),
        input_output_aliases={1 + k: v for k, v in (aliases or {}).items()},
        cost_estimate=pl.CostEstimate(
            flops=0, bytes_accessed=int(us * 3.4e6), transcendentals=0
        ),
        compiler_params=pltpu.CompilerParams(vmem_limit_bytes=12 * 1024 * 1024),
    )(*arrays)


def columns_of(ref, block, width):
    return ref.at[:, pl.ds(pl.multiple_of(block * width, width), width)]


def start(src, dst, sem):
    copy = pltpu.make_async_copy(src, dst, sem)
    copy.start()
    return copy


def turned(at, s, src, dst, sems, base, first=0):
    return [
        start(
            columns_of(src, s[at["heads"] + k], HEAD),
            dst.at[:, pl.ds(first + k * HEAD, HEAD)],
            sems.at[base + k],
        )
        for k in range(src.shape[1] // HEAD)
    ]


def ready_body(at, s, w, act, cot, *rest):
    *lows, w_v, packed, sems = rest
    rows = w.shape[0]
    step = rows // 4
    heads = w.shape[1] // HEAD
    wide = packed.shape[1] - cot.shape[1]
    first = [
        turned(
            at, s, w.at[pl.ds(i * step, step)], w_v.at[pl.ds(i * step, step)], sems, i * heads
        )
        for i in range(4)
    ]
    copies = [
        start(
            columns_of(act, 2 * d + 1 - s[at["core"]], rows),
            packed.at[:, pl.ds(d * rows, rows)],
            sems.at[4 * heads + d],
        )
        for d in range(wide // rows)
    ]
    copies += turned(at, s, cot, packed, sems, 4 * heads + len(copies), wide)
    for i in range(4):
        for copy in first[i]:
            copy.wait()
        here = pl.ds(i * step, step)
        for (offset, part), low in zip(PARTS, lows):
            low[here, :] = w_v[here, offset : offset + part].astype(BF16)
    for copy in copies:
        copy.wait()


def own_body(at, s, packed, act, anchor, moment, *rest):
    sums_ref, anchor_out, moment_out, act_s, held, sems = rest
    chips, _, rows = act_s.shape
    blocks = [
        start(columns_of(act, 2 * d + s[at["core"]], rows), act_s.at[d], sems.at[d])
        for d in range(chips)
    ]
    loads = [
        start(src, held.at[k], sems.at[chips + k]) for k, src in enumerate((anchor, moment))
    ]
    stores = []
    for d in range(chips):
        blocks[d].wait()
        for i in range(rows // TILE):
            sums_ref[pl.ds(d * rows + i * TILE, TILE), :] = rows_by_columns(
                act_s[d, :, i * TILE : (i + 1) * TILE], packed[:, chips * rows :]
            )
        if d == 1:
            for k, dst in enumerate((anchor_out, moment_out)):
                loads[k].wait()
                stores.append(start(held.at[k], dst, sems.at[chips + 2 + k]))
    for copy in stores:
        copy.wait()


def sibling_body(at, s, before, packed, m, v, anchor, moment, *rest):
    sums_ref, m_v, v_v, anchor_v, moment_v, sems = rest
    copies = []
    for src, dst in ((m, m_v), (v, v_v)):
        copies += turned(at, s, src, dst, sems, len(copies))
    for src, dst in ((anchor, anchor_v), (moment, moment_v)):
        copies.append(start(columns_of(src, s[at["heads"]], HEAD), dst, sems.at[len(copies)]))
    wide = sums_ref.shape[0]
    for i in range(wide // TILE):
        here = slice(i * TILE, (i + 1) * TILE)
        sums_ref[here, :] = before[here, :] + rows_by_columns(packed[:, here], packed[:, wide:])
    for copy in copies:
        copy.wait()


def hop_body(at, step, offset, s, sums_ref, from_o, from_e, *rest):
    to_e, to_o, picked = rest[-3:]
    older = rest[0] if step == 3 else None
    rows, part = to_e.shape
    columns = slice(offset, offset + part)
    base = at["hop"] + 4 * (step - 1)
    size = 64

    def each(body):
        @pl.loop(0, rows // size, unroll=4)
        def _(i):
            body(pl.multiple_of(i * size, size))

    for mode, block, src, dst in (
        (s[base], s[base + 1], from_o, to_e),
        (s[base + 2], s[base + 3], from_e, to_o),
    ):
        first = pl.multiple_of(block * rows, rows)

        @pl.when(mode == 0)
        def _():
            def body(r):
                dst[pl.ds(r, size), :] = sums_ref[pl.ds(first + r, size), columns].astype(BF16)

            each(body)

        @pl.when(mode == 1)
        def _():
            def body(r):
                here = pl.ds(r, size)
                added = src[here, :].astype(F32) + sums_ref[pl.ds(first + r, size), columns]
                dst[here, :] = added.astype(BF16)

            each(body)

        @pl.when(mode == 2)
        def _():
            def body(r):
                dst[pl.ds(r, size), :] = src[pl.ds(r, size), :]

            each(body)

    def keep(src):
        def body(r):
            picked[pl.ds(r, size), :] = src[pl.ds(r, size), :]

        each(body)

    if step == 1:
        keep(from_e)
    else:

        @pl.when(s[at["middle"]] == 1)
        def _():
            keep(from_o if older is None else older)

        @pl.when(s[at["middle"]] == 0)
        def _():
            keep(from_e)


def grad_body(at, which, s, packed, packed_sib, *rest):
    theirs, out, token, stage, sems = rest[-5:]
    rows = stage.shape[1]
    wide = packed.shape[1] - sum(part for _, part in PARTS)
    copies = []
    if which > 0:
        copies.append(
            start(
                rest[len(PARTS)], columns_of(out, s[at["grad"] + 2 * which - 1], rows), sems.at[1]
            )
        )
    for cot, dst in ((packed_sib, theirs), (packed, stage)):
        for i in range(rows // TILE):
            here = slice(i * TILE, (i + 1) * TILE)
            total = None
            for (offset, part), block in zip(PARTS, rest):
                term = lax.dot_general(
                    cot[:, wide + offset : wide + offset + part],
                    block[here, :],
                    (((1,), (1,)), ((), ())),
                    preferred_element_type=F32,
                )
                total = term if total is None else total + term
            dst[:, here] = total.astype(BF16)
    copies.append(start(stage, columns_of(out, s[at["grad"] + 2 * which], rows), sems.at[0]))
    token[...] = jnp.zeros_like(token)
    for copy in copies:
        copy.wait()


def adam_body(at, offset, s, sums_ref, from_e, from_o, w, m, v, *rest):
    stage, sems = rest[-2:]
    rows, part = from_e.shape
    if offset == 0:
        anchor, diff = rest[0], rest[4]
        outs = rest[1:4]
    else:
        outs = rest[3:6]
    columns = slice(offset, offset + part)
    size = 64 * 256 // part // 16 * 16
    base = pl.multiple_of(s[at["z"]] * rows, rows)
    copies = []
    for tile in range(rows // TILE):

        @pl.loop(0, TILE // size)
        def _(i):
            r = pl.multiple_of(tile * TILE + i * size, size)
            here = pl.ds(r, size)
            one = sums_ref[pl.ds(base + r, size), columns] + from_e[here, :].astype(F32)
            gradient = jnp.where(s[at["middle"]] == 1, one + from_o[here, :].astype(F32), one)
            weights = w[here, columns]
            first = 0.9 * m[here, columns] + 0.1 * gradient
            second = 0.95 * v[here, columns] + 0.05 * gradient * gradient
            update = first / CORR_ONE / (jnp.sqrt(second / CORR_TWO) + 1e-08) + 0.1 * weights
            stepped = weights - 0.1 * update
            stage[0, here, :] = stepped
            stage[1, here, :] = first
            stage[2, here, :] = second
            if offset == 0:
                diff[here, :] = (anchor[here, :] - stepped[:, :HEAD]).astype(BF16)

        there = pl.ds(tile * TILE, TILE)
        for k, out in enumerate(outs):
            for h in range(part // HEAD):
                copies.append(
                    start(
                        stage.at[k, there, pl.ds(h * HEAD, HEAD)],
                        columns_of(out.at[there], s[at["heads"] + offset // HEAD + h], HEAD),
                        sems.at[len(copies)],
                    )
                )
    for copy in copies:
        copy.wait()


def outer_body(at, s, own, one, two, three, anchor, moment, theirs, *rest):
    inner, new_anchor, new_moment, grads, stage, sems = rest[4:]
    rows = theirs.shape[1]
    copies = [start(theirs, columns_of(grads, s[at["grad"] + 7], rows), sems.at[3])]
    total = (own[...].astype(F32) + one[...].astype(F32)) + (
        two[...].astype(F32) + three[...].astype(F32)
    )
    average = total / 4.0
    momentum = 0.9 * moment[...] + average
    stage[0] = momentum
    stage[1] = anchor[...] - 0.7 * (average + 0.9 * momentum)
    copies += [
        start(stage.at[k], columns_of(out, s[at["heads"]], HEAD), sems.at[i])
        for i, (k, out) in enumerate(((0, new_moment), (1, new_anchor), (1, inner)))
    ]
    for copy in copies:
        copy.wait()


def line(
    activations,
    cotangent,
    inner_weights,
    first_moment,
    second_moment,
    anchor,
    outer_momentum,
    fragment,
):
    act, cot, weights = activations[0], cotangent[0], inner_weights[0]
    moment, second = first_moment[0], second_moment[0]
    tokens, width = act.shape
    rows, columns = weights.shape
    chips = lax.axis_size("fsdp") // 2
    me = lax.axis_index("fsdp")
    z, core = me // 2, me % 2
    head = fragment[0]
    last = chips - 1
    middle = (z > 0) & (z < last)
    even = z % 2 == 0
    zd = last - z

    def cross(i):
        return i ^ 1 if i // 2 in (0, last) else (i + 2 if i // 2 % 2 else i - 2)

    e_perm = [(i, i ^ 2) for i in range(2 * chips)]
    o_perm = [(i, cross(i)) for i in range(2 * chips)]
    swap = [(i, i ^ 1) for i in range(2 * chips)]

    values, at = [], {}

    def name(key, *numbers):
        at[key] = len(values)
        values.extend(jnp.asarray(v, jnp.int32) for v in numbers)

    name("z", z)
    name("core", core)
    name("middle", middle)
    name("heads", *[(head + k) % (columns // HEAD) for k in range(columns // HEAD)])
    name("grad", *[2 * (z ^ k) + c for k in range(chips) for c in (core, 1 - core)])
    hops = []
    for step in range(1, chips):
        up_mode = jnp.where(step <= z, 2, jnp.where(z == 0, 0, 1))
        down_mode = jnp.where(step <= zd, 2, jnp.where(zd == 0, 0, 1))
        up_to = jnp.clip(chips - step + z, 0, last)
        down_to = jnp.clip(step - 1 - zd, 0, last)
        hops += [
            jnp.where(even, up_mode, down_mode),
            jnp.where(even, up_to, down_to),
            jnp.where(middle, jnp.where(even, down_mode, up_mode), 2),
            jnp.where(even, down_to, up_to),
        ]
    name("hop", *hops)
    s = jnp.stack(values)

    def permute(x, perm, axis="fsdp"):
        return lax.ppermute(x, axis, perm)

    dma = pltpu.SemaphoreType.DMA
    from_e, from_o = [[]], [[]]
    heads = columns // HEAD
    *low, w_v, packed = call(
        functools.partial(ready_body, at),
        s,
        [weights, act, cot],
        [vmem(rows, part, dtype=BF16) for _, part in PARTS]
        + [vmem(rows, columns), vmem(tokens, chips * rows + columns, dtype=BF16)],
        [dma((5 * heads + chips,))],
        us=3.0,
    )
    for x in low:
        from_e[0].append(permute(x, e_perm))
        from_o[0].append(permute(x, o_perm))
    packed_sib = permute(packed, swap)

    sums_shape = vmem(chips * rows, columns)
    sums_own, new_anchor, new_momentum = call(
        functools.partial(own_body, at),
        s,
        [Held(packed), act, anchor, outer_momentum],
        [sums_shape, hbm(rows, columns), hbm(rows, columns)],
        [vmem(chips, tokens, rows, dtype=BF16), vmem(2, rows, columns), dma((chips + 4,))],
        us=5.0,
    )
    sums_both, m_v, v_v, anchor_v, moment_v = call(
        functools.partial(sibling_body, at),
        s,
        [Held(sums_own), Held(packed_sib), moment, second, anchor, outer_momentum],
        [sums_shape] + [vmem(rows, columns)] * 2 + [vmem(rows, HEAD)] * 2,
        [dma((2 * heads + 2,))],
        {0: 0},
        us=5.0,
    )

    def hop(step, j, after):
        offset, part = PARTS[j]
        ins = [Held(sums_both), Held(from_o[step - 1][j]), Held(from_e[step - 1][j])]
        if step == 3:
            ins += [Held(from_o[0][j])]
        return call(
            functools.partial(hop_body, at, step, offset),
            s,
            ins,
            [vmem(rows, part, dtype=BF16)] * 3,
            after=after,
        )

    def grad(which, before, own, after):
        ins = [Held(x) for x in [packed, packed_sib, *own]]
        aliases = {}
        if before is not None:
            theirs, buffer = before
            ins += [Held(theirs)]
            aliases = {len(ins): 1}
            ins += [buffer]
        theirs, buffer, token = call(
            functools.partial(grad_body, at, which),
            s,
            ins,
            [
                vmem(tokens, rows, dtype=BF16),
                hbm(tokens, width, dtype=BF16),
                vmem(8, 128),
            ],
            [vmem(tokens, rows, dtype=BF16), dma((2,))],
            aliases,
            after,
            us=2.1,
        )
        return (permute(theirs, swap), buffer), token

    grads, after, picked = None, (), low
    for step in range(1, chips):
        from_e.append([])
        from_o.append([])
        found = []
        for j in range(len(PARTS)):
            to_e, to_o, pick = hop(step, j, after)
            from_e[step].append(permute(to_e, e_perm))
            from_o[step].append(permute(to_o, o_perm))
            found.append(pick)
            after = ()
            if j == 0:
                grads, token = grad(step - 1, grads, picked, (to_e,))
                after = (token,)
        picked = found
    grads, token = grad(last, grads, picked, ())

    state, diff, others = None, None, None
    for j, (offset, part) in enumerate(PARTS):
        ins = [sums_both, from_e[last][j], from_o[last][j], w_v, m_v, v_v]
        outs = [hbm(rows, columns)] * 3
        aliases, after = {}, ()
        if j == 0:
            ins += [anchor_v]
            outs = outs + [vmem(rows, HEAD, dtype=BF16)]
            after = (token,)
        ins = [Held(x) for x in ins]
        if j > 0:
            aliases = {len(ins) + k: k for k in range(3)}
            ins += state
        result = call(
            functools.partial(adam_body, at, offset),
            s,
            ins,
            outs,
            [vmem(3, rows, part), dma((3 * rows // TILE * part // HEAD,))],
            aliases,
            after,
            us=2.8,
        )
        state = list(result[:3])
        if j == 0:
            diff = result[3]
            others = [permute(diff, [(i, i ^ k) for i in range(4)], "group") for k in (1, 2, 3)]
    inner, new_anchor, new_momentum, input_grad = call(
        functools.partial(outer_body, at),
        s,
        [Held(x) for x in [diff, *others, anchor_v, moment_v, grads[0]]]
        + [state[0], new_anchor, new_momentum, grads[1]],
        [hbm(rows, columns)] * 3 + [hbm(tokens, width, dtype=BF16)],
        [vmem(2, rows, HEAD), dma((4,))],
        {7: 0, 8: 1, 9: 2, 10: 3},
        us=2.0,
    )
    return input_grad[None], inner[None], state[1][None], state[2][None], new_anchor, new_momentum


def solution(mesh):
    in_specs = (
        P("group", "fsdp", None),
        P("group", "fsdp", None),
        P("group", "fsdp", None),
        P("group", "fsdp", None),
        P("group", "fsdp", None),
        P("fsdp", None),
        P("fsdp", None),
        P(),
    )
    out_specs = (
        P("group", "fsdp", None),
        P("group", "fsdp", None),
        P("group", "fsdp", None),
        P("group", "fsdp", None),
        P("fsdp", None),
        P("fsdp", None),
    )
    short = mesh.shape["fsdp"] == 8 and mesh.shape["group"] == 4
    return jax.shard_map(
        line if short else plain,
        mesh=mesh,
        in_specs=in_specs,
        out_specs=out_specs,
        check_vma=False,
    )
```

```python
import functools

import jax
import jax.numpy as jnp
from jax import lax
from jax.experimental import pallas as pl
from jax.experimental.pallas import tpu as pltpu
from jax.sharding import PartitionSpec as P

HEAD = 128
STEP = 100
CORR_ONE = 1.0 - 0.9**STEP
CORR_TWO = 1.0 - 0.95**STEP
PARTS = ((0, 256), (256, 256))
TILE = 256
BF16 = jnp.bfloat16
F32 = jnp.float32


def plain(
    activations,
    cotangent,
    inner_weights,
    first_moment,
    second_moment,
    anchor,
    outer_momentum,
    fragment,
):
    tokens_in = activations[0]
    upstream = cotangent[0]
    weights = inner_weights[0]
    low_weights = weights.astype(BF16)
    input_grad = lax.dot_general(
        upstream,
        lax.all_gather(low_weights, "fsdp", axis=0, tiled=True),
        (((1,), (1,)), ((), ())),
        preferred_element_type=F32,
    ).astype(BF16)
    gradient = lax.psum_scatter(
        lax.dot_general(tokens_in, upstream, (((0,), (0,)), ((), ())), preferred_element_type=F32),
        "fsdp",
        scatter_dimension=0,
        tiled=True,
    )
    new_first = 0.9 * first_moment[0] + 0.1 * gradient
    new_second = 0.95 * second_moment[0] + 0.05 * gradient * gradient
    update = new_first / CORR_ONE / (jnp.sqrt(new_second / CORR_TWO) + 1e-08) + 0.1 * weights
    stepped = weights - 0.1 * update
    offset = fragment[0] * HEAD
    local_cols = lax.dynamic_slice_in_dim(stepped, offset, HEAD, 1)
    anchor_cols = lax.dynamic_slice_in_dim(anchor, offset, HEAD, 1)
    moment_cols = lax.dynamic_slice_in_dim(outer_momentum, offset, HEAD, 1)
    summed = lax.psum((anchor_cols - local_cols).astype(BF16), "group").astype(F32)
    average = summed / lax.axis_size("group")
    moment_new = 0.9 * moment_cols + average
    anchor_next = anchor_cols - 0.7 * (average + 0.9 * moment_new)
    new_momentum = lax.dynamic_update_slice_in_dim(outer_momentum, moment_new, offset, 1)
    new_anchor = lax.dynamic_update_slice_in_dim(anchor, anchor_next, offset, 1)
    new_inner = lax.dynamic_update_slice_in_dim(stepped, anchor_next, offset, 1)
    return (
        input_grad[None],
        new_inner[None],
        new_first[None],
        new_second[None],
        new_anchor,
        new_momentum,
    )


def rows_by_columns(act, cot):
    return lax.dot_general(act, cot, (((0,), (0,)), ((), ())), preferred_element_type=F32)


def vmem(*shape, dtype=F32):
    return pltpu.VMEM(shape, dtype)


def hbm(*shape, dtype=F32):
    return jax.ShapeDtypeStruct(shape, dtype)


class Held:
    def __init__(self, array):
        self.array = array


def call(body, scalars, ins, outs, scratch=(), aliases=None, after=(), us=1.0):
    arrays, specs = [scalars], [pl.BlockSpec(memory_space=pltpu.SMEM)]
    for x in ins:
        if isinstance(x, Held):
            arrays.append(pltpu.with_memory_space_constraint(x.array, pltpu.VMEM))
            specs.append(pl.BlockSpec(memory_space=pltpu.VMEM))
        else:
            arrays.append(pltpu.with_memory_space_constraint(x, pltpu.HBM))
            specs.append(pl.BlockSpec(memory_space=pltpu.HBM))
    first = len(arrays)
    arrays += [pltpu.with_memory_space_constraint(x, pltpu.VMEM) for x in after]
    specs += [pl.BlockSpec(memory_space=pltpu.VMEM)] * len(after)

    def inner(*refs):
        body(*refs[:first], *refs[first + len(after) :])

    return pl.pallas_call(
        inner,
        in_specs=specs,
        out_specs=[
            pl.BlockSpec(memory_space=pl.ANY if isinstance(o, jax.ShapeDtypeStruct) else pltpu.VMEM)
            for o in outs
        ],
        out_shape=list(outs),
        scratch_shapes=list(scratch),
        input_output_aliases={1 + k: v for k, v in (aliases or {}).items()},
        cost_estimate=pl.CostEstimate(
            flops=0, bytes_accessed=int(us * 3.4e6), transcendentals=0
        ),
        compiler_params=pltpu.CompilerParams(vmem_limit_bytes=12 * 1024 * 1024),
    )(*arrays)


def columns_of(ref, block, width):
    return ref.at[:, pl.ds(pl.multiple_of(block * width, width), width)]


def start(src, dst, sem):
    copy = pltpu.make_async_copy(src, dst, sem)
    copy.start()
    return copy


def pieces(head):
    return (0, HEAD, head), (HEAD, HEAD, head ^ 1), (2 * HEAD, 2 * HEAD, 1 - head // 2)


def turned(at, s, src, dst, sems, base, first=0):
    return [
        start(
            columns_of(src, s[at["pieces"] + k], width),
            dst.at[:, pl.ds(column + first, width)],
            sems.at[base + k],
        )
        for k, (column, width, _) in enumerate(pieces(0))
    ]


def cast_body(offset, s, w, low, wide, sems):
    rows, part = low.shape
    step = rows // 2
    copies = [
        start(
            w.at[pl.ds(i * step, step), pl.ds(offset, part)],
            wide.at[pl.ds(i * step, step)],
            sems.at[i],
        )
        for i in range(2)
    ]
    for i, copy in enumerate(copies):
        copy.wait()

        @pl.loop(0, step // 64)
        def _(n):
            here = pl.ds(pl.multiple_of(i * step + n * 64, 64), 64)
            low[here, :] = wide[here, :].astype(BF16)


def load_blocks(at, s, act, cot, act_s, cot_v, sems):
    heads = turned(at, s, cot, cot_v, sems, 0)
    rows = act_s.shape[2]
    blocks = [
        start(columns_of(act, 2 * d + s[at["core"]], rows), act_s.at[d], sems.at[len(heads) + d])
        for d in range(act_s.shape[0])
    ]
    return heads, blocks


def own_body(at, s, act, cot, anchor, moment, *rest):
    sums_ref, anchor_out, moment_out, act_s, cot_v, held, sems = rest
    chips, _, rows = act_s.shape
    heads, blocks = load_blocks(at, s, act, cot, act_s, cot_v, sems)
    base = len(heads) + chips
    loads = [start(src, held.at[k], sems.at[base + k]) for k, src in enumerate((anchor, moment))]
    stores = []
    for k, dst in enumerate((anchor_out, moment_out)):
        loads[k].wait()
        stores.append(start(held.at[k], dst, sems.at[base + 2 + k]))
    for copy in heads + blocks:
        copy.wait()

    @pl.loop(0, chips)
    def _(d):
        for i in range(rows // TILE):
            here = pl.ds(pl.multiple_of(d * rows + i * TILE, TILE), TILE)
            sums_ref[here, :] = rows_by_columns(
                act_s[d, :, i * TILE : (i + 1) * TILE], cot_v[...]
            )

    for copy in stores:
        copy.wait()


def sibling_body(at, s, before, act, cot, w, m, v, anchor, moment, *rest):
    sums_ref, w_v, m_v, v_v, anchor_v, moment_v, act_s, cot_v, sems = rest
    chips, _, rows = act_s.shape
    heads, blocks = load_blocks(at, s, act, cot, act_s, cot_v, sems)
    base = len(heads) + chips
    copies = []
    for src, dst in ((w, w_v), (m, m_v), (v, v_v)):
        copies += turned(at, s, src, dst, sems, base + len(copies))
    for src, dst in ((anchor, anchor_v), (moment, moment_v)):
        copies.append(
            start(columns_of(src, s[at["pieces"]], HEAD), dst, sems.at[base + len(copies)])
        )
    for copy in heads + blocks:
        copy.wait()

    @pl.loop(0, chips)
    def _(d):
        for i in range(rows // TILE):
            here = pl.ds(pl.multiple_of(d * rows + i * TILE, TILE), TILE)
            sums_ref[here, :] = before[here, :] + rows_by_columns(
                act_s[d, :, i * TILE : (i + 1) * TILE], cot_v[...]
            )

    for copy in copies:
        copy.wait()


def hop_body(at, step, offset, s, sums_ref, from_o, from_e, *rest):
    to_e, to_o, picked = rest[-3:]
    older = rest[0] if step == 3 else None
    rows, part = to_e.shape
    columns = slice(offset, offset + part)
    base = at["hop"] + 4 * (step - 1)
    size = 64

    def each(body):
        @pl.loop(0, rows // size)
        def _(i):
            body(pl.multiple_of(i * size, size))

    for mode, block, src, dst in (
        (s[base], s[base + 1], from_o, to_e),
        (s[base + 2], s[base + 3], from_e, to_o),
    ):
        first = pl.multiple_of(block * rows, rows)

        @pl.when(mode == 0)
        def _():
            def body(r):
                dst[pl.ds(r, size), :] = sums_ref[pl.ds(first + r, size), columns].astype(BF16)

            each(body)

        @pl.when(mode == 1)
        def _():
            def body(r):
                here = pl.ds(r, size)
                added = src[here, :].astype(F32) + sums_ref[pl.ds(first + r, size), columns]
                dst[here, :] = added.astype(BF16)

            each(body)

        @pl.when(mode == 2)
        def _():
            def body(r):
                dst[pl.ds(r, size), :] = src[pl.ds(r, size), :]

            each(body)

    def keep(src):
        def body(r):
            picked[pl.ds(r, size), :] = src[pl.ds(r, size), :]

        each(body)

    if step == 1:
        keep(from_e)
    else:

        @pl.when(s[at["middle"]] == 1)
        def _():
            keep(from_o if older is None else older)

        @pl.when(s[at["middle"]] == 0)
        def _():
            keep(from_e)


def grad_body(at, which, s, cot_own, cot_sib, *rest):
    theirs, out, token, stage, sems = rest[-5:]
    rows = stage.shape[1]
    copies = []
    if which > 0:
        copies.append(
            start(
                rest[len(PARTS)], columns_of(out, s[at["grad"] + 2 * which - 1], rows), sems.at[1]
            )
        )
    for cot, dst in ((cot_sib, theirs), (cot_own, stage)):
        for i in range(rows // TILE):
            here = slice(i * TILE, (i + 1) * TILE)
            total = None
            for (offset, part), block in zip(PARTS, rest):
                term = lax.dot_general(
                    cot[:, offset : offset + part],
                    block[here, :],
                    (((1,), (1,)), ((), ())),
                    preferred_element_type=F32,
                )
                total = term if total is None else total + term
            dst[:, here] = total.astype(BF16)
    copies.append(start(stage, columns_of(out, s[at["grad"] + 2 * which], rows), sems.at[0]))
    token[...] = jnp.zeros_like(token)
    for copy in copies:
        copy.wait()


def adam(at, offset, first_row, s, sums_ref, from_e, from_o, w, m, v, put, count, width, taken):
    columns = slice(offset, offset + width)
    size = 128
    base = pl.multiple_of(s[at["z"]] * from_e.shape[0], TILE)

    @pl.loop(0, count // size)
    def _(i):
        r = pl.multiple_of(first_row + i * size, size)
        here = pl.ds(r, size)
        one = sums_ref[pl.ds(base + r, size), columns] + from_e[here, taken].astype(F32)
        both = one + from_o[here, taken].astype(F32)
        gradient = jnp.where(s[at["middle"]] == 1, both, one)
        first = 0.9 * m[here, columns] + 0.1 * gradient
        second = 0.95 * v[here, columns] + 0.05 * gradient * gradient
        scaled = second * (1.0 / CORR_TWO)
        below = scaled * lax.rsqrt(scaled) + 1e-08
        over = pl.reciprocal(below, approx=True)
        over = over * (2.0 - below * over)
        stepped = (1.0 - 0.1 * 0.1) * w[here, columns] - first * (0.1 / CORR_ONE) * over
        put(r, stepped, first, second)


def head_body(at, s, sums_ref, from_e, from_o, w, m, v, anchor, upper, lower, first_v, second_v):
    rows = anchor.shape[0]
    for k, diff in enumerate((upper, lower)):
        top = k * rows // 2

        def put(r, stepped, first, second):
            here = pl.ds(r, stepped.shape[0])
            first_v[here, :] = first
            second_v[here, :] = second
            there = pl.ds(r - top, stepped.shape[0])
            diff[there, :] = (anchor[here, :] - stepped).astype(BF16)

        args = (from_e, from_o, w, m, v, put, rows // 2, HEAD, slice(0, HEAD))
        adam(at, 0, top, s, sums_ref, *args)


def rest_body(at, offset, part, within, s, sums_ref, from_e, from_o, w, m, v, *rest):
    stage, sems = rest[-2:]
    rows = from_e.shape[0]
    copies = []
    if within:
        first_v, second_v, theirs = rest[:3]
        *outs, grads, token = rest[4:-2]
        for k, src in enumerate((first_v, second_v)):
            there = columns_of(outs[1 + k], s[at["pieces"]], HEAD)
            copies.append(start(src, there, sems.at[k]))
        copies.append(start(theirs, columns_of(grads, s[at["grad"] + 7], rows), sems.at[2]))
    else:
        *outs, token = rest[3:-2]
    token[...] = jnp.zeros_like(token)
    piece = next(k for k, (column, *_) in enumerate(pieces(0)) if column == offset)

    def put(r, stepped, first, second):
        here = pl.ds(r, stepped.shape[0])
        stage[0, here, :] = stepped
        stage[1, here, :] = first
        stage[2, here, :] = second

    for tile in range(rows // TILE):
        args = (from_e, from_o, w, m, v, put, TILE, part, slice(within, within + part))
        adam(at, offset, tile * TILE, s, sums_ref, *args)
        there = pl.ds(tile * TILE, TILE)
        for k, out in enumerate(outs):
            copies.append(
                start(
                    stage.at[k, there],
                    columns_of(out.at[there], s[at["pieces"] + piece], part),
                    sems.at[len(copies)],
                )
            )
    for copy in copies:
        copy.wait()


def mix_body(s, own, other, out):
    out[...] = (own[...].astype(F32) + other[...].astype(F32)).astype(BF16)


def outer_body(at, s, upper, upper_in, lower, lower_in, anchor, moment, *rest):
    inner, new_anchor, new_moment, stage, sems = rest[3:]
    half = upper.shape[0]
    copies = []
    for n, (own, other) in enumerate(((upper, upper_in), (lower, lower_in))):
        here = pl.ds(n * half, half)
        average = (own[...].astype(F32) + other[...].astype(F32)) / 4.0
        momentum = 0.9 * moment[here, :] + average
        stage[0, here, :] = momentum
        stage[1, here, :] = anchor[here, :] - 0.7 * (average + 0.9 * momentum)
        copies += [
            start(
                stage.at[k, here], columns_of(out.at[here], s[at["pieces"]], HEAD), sems.at[3 * n + i]
            )
            for i, (k, out) in enumerate(((0, new_moment), (1, new_anchor), (1, inner)))
        ]
    for copy in copies:
        copy.wait()


def line(
    activations,
    cotangent,
    inner_weights,
    first_moment,
    second_moment,
    anchor,
    outer_momentum,
    fragment,
):
    act, cot, weights = activations[0], cotangent[0], inner_weights[0]
    moment, second = first_moment[0], second_moment[0]
    tokens, width = act.shape
    rows, columns = weights.shape
    chips = lax.axis_size("fsdp") // 2
    me = lax.axis_index("fsdp")
    z, core = me // 2, me % 2
    head = fragment[0]
    last = chips - 1
    middle = (z > 0) & (z < last)
    even = z % 2 == 0
    zd = last - z

    def cross(i):
        return i ^ 1 if i // 2 in (0, last) else (i + 2 if i // 2 % 2 else i - 2)

    e_perm = [(i, i ^ 2) for i in range(2 * chips)]
    o_perm = [(i, cross(i)) for i in range(2 * chips)]
    swap = [(i, i ^ 1) for i in range(2 * chips)]
    x_perm, y_perm = [(i, i ^ 1) for i in range(4)], [(i, i ^ 2) for i in range(4)]

    values, at = [], {}

    def name(key, *numbers):
        at[key] = len(values)
        values.extend(jnp.asarray(v, jnp.int32) for v in numbers)

    name("z", z)
    name("core", core)
    name("middle", middle)
    name("pieces", *[block for _, _, block in pieces(head)])
    name("grad", *[2 * (z ^ k) + c for k in range(chips) for c in (core, 1 - core)])
    hops = []
    for step in range(1, chips):
        up_mode = jnp.where(step <= z, 2, jnp.where(z == 0, 0, 1))
        down_mode = jnp.where(step <= zd, 2, jnp.where(zd == 0, 0, 1))
        up_to = jnp.clip(chips - step + z, 0, last)
        down_to = jnp.clip(step - 1 - zd, 0, last)
        hops += [
            jnp.where(even, up_mode, down_mode),
            jnp.where(even, up_to, down_to),
            jnp.where(middle, jnp.where(even, down_mode, up_mode), 2),
            jnp.where(even, down_to, up_to),
        ]
    name("hop", *hops)
    s = jnp.stack(values)

    def permute(x, perm, axis="fsdp"):
        return lax.ppermute(x, axis, perm)

    dma = pltpu.SemaphoreType.DMA
    from_e, from_o = [[]], [[]]
    act_sib, cot_sib = permute(act, swap), permute(cot, swap)
    (_, first), (offset, part) = PARTS
    low = [weights[:, :first].astype(BF16)]
    low += call(
        functools.partial(cast_body, offset),
        s,
        [weights],
        [vmem(rows, part, dtype=BF16)],
        [vmem(rows, part), dma((2,))],
        after=[cot_sib],
        us=2.0,
    )
    for x in low:
        from_e[0].append(permute(x, e_perm))
        from_o[0].append(permute(x, o_perm))

    sums_shape = vmem(chips * rows, columns)
    cot_shape = vmem(tokens, columns, dtype=BF16)
    block_shape = vmem(chips, tokens, rows, dtype=BF16)
    sums_own, new_anchor, new_momentum = call(
        functools.partial(own_body, at),
        s,
        [act, Held(cot), anchor, outer_momentum],
        [sums_shape, hbm(rows, columns), hbm(rows, columns)],
        [block_shape, cot_shape, vmem(2, rows, columns), dma((chips + 7,))],
        after=low[-1:],
        us=5.0,
    )
    sums_both, w_v, m_v, v_v, anchor_v, moment_v = call(
        functools.partial(sibling_body, at),
        s,
        [Held(sums_own), act_sib, Held(cot_sib), weights, moment, second, anchor, outer_momentum],
        [sums_shape] + [vmem(rows, columns)] * 3 + [vmem(rows, HEAD)] * 2,
        [block_shape, cot_shape, dma((chips + 14,))],
        {0: 0},
        us=5.0,
    )

    def hop(step, j, after):
        offset, part = PARTS[j]
        ins = [Held(sums_both), Held(from_o[step - 1][j]), Held(from_e[step - 1][j])]
        if step == 3:
            ins += [Held(from_o[0][j])]
        return call(
            functools.partial(hop_body, at, step, offset),
            s,
            ins,
            [vmem(rows, part, dtype=BF16)] * 3,
            after=after,
        )

    def grad(which, before, own, after):
        ins = [Held(x) for x in [cot, cot_sib, *own]]
        aliases = {}
        if before is not None:
            theirs, buffer = before
            ins += [Held(theirs)]
            aliases = {len(ins): 1}
            ins += [buffer]
        theirs, buffer, token = call(
            functools.partial(grad_body, at, which),
            s,
            ins,
            [
                vmem(tokens, rows, dtype=BF16),
                hbm(tokens, width, dtype=BF16),
                vmem(8, 128),
            ],
            [vmem(tokens, rows, dtype=BF16), dma((2,))],
            aliases,
            after,
            us=2.1,
        )
        return (permute(theirs, swap), buffer), token

    grads, after, picked = None, (), low
    for step in range(1, chips):
        from_e.append([])
        from_o.append([])
        found = []
        for j in range(len(PARTS)):
            to_e, to_o, pick = hop(step, j, after)
            from_e[step].append(permute(to_e, e_perm))
            from_o[step].append(permute(to_o, o_perm))
            found.append(pick)
            after = ()
            if j == 0:
                grads, token = grad(step - 1, grads, picked, (to_e,))
                after = (token,)
        picked = found
    grads, token = grad(last, grads, picked, ())

    theirs, input_grad = grads
    half = vmem(rows // 2, HEAD, dtype=BF16)
    full = [hbm(rows, columns)] * 3

    def inputs(j):
        return [sums_both, from_e[last][j], from_o[last][j], w_v, m_v, v_v]

    upper, lower, first_v, second_v = call(
        functools.partial(head_body, at),
        s,
        [Held(x) for x in [*inputs(0), anchor_v]],
        [half, half, vmem(rows, HEAD), vmem(rows, HEAD)],
        after=(token,),
        us=1.0,
    )
    upper_in = permute(upper, x_perm, "group")
    lower_in = permute(lower, y_perm, "group")
    *state, input_grad, token = call(
        functools.partial(rest_body, at, HEAD, PARTS[0][1] - HEAD, HEAD),
        s,
        [Held(x) for x in [*inputs(0), first_v, second_v, theirs]] + [input_grad],
        full + [hbm(tokens, width, dtype=BF16), vmem(8, 128)],
        [vmem(3, rows, PARTS[0][1] - HEAD), dma((3 + 3 * rows // TILE,))],
        {9: 3},
        us=2.0,
    )
    upper = call(mix_body, s, [Held(upper), Held(upper_in)], [half], after=(token,), us=0.5)[0]
    upper_in = permute(upper, y_perm, "group")
    lower = call(mix_body, s, [Held(lower), Held(lower_in)], [half], after=(upper,), us=0.5)[0]
    lower_in = permute(lower, x_perm, "group")
    pairs = [upper, upper_in, lower, lower_in]
    offset, part = PARTS[1]
    *state, token = call(
        functools.partial(rest_body, at, offset, part, 0),
        s,
        [Held(x) for x in inputs(1)] + state,
        full + [vmem(8, 128)],
        [vmem(3, rows, part), dma((3 * rows // TILE,))],
        {6: 0, 7: 1, 8: 2},
        after=(lower,),
        us=3.0,
    )
    inner, new_anchor, new_momentum = call(
        functools.partial(outer_body, at),
        s,
        [Held(x) for x in [*pairs, anchor_v, moment_v]] + [state[0], new_anchor, new_momentum],
        [hbm(rows, columns)] * 3,
        [vmem(2, rows, HEAD), dma((6,))],
        {6: 0, 7: 1, 8: 2},
        us=2.0,
    )
    return input_grad[None], inner[None], state[1][None], state[2][None], new_anchor, new_momentum


def solution(mesh):
    in_specs = (
        P("group", "fsdp", None),
        P("group", "fsdp", None),
        P("group", "fsdp", None),
        P("group", "fsdp", None),
        P("group", "fsdp", None),
        P("fsdp", None),
        P("fsdp", None),
        P(),
    )
    out_specs = (
        P("group", "fsdp", None),
        P("group", "fsdp", None),
        P("group", "fsdp", None),
        P("group", "fsdp", None),
        P("fsdp", None),
        P("fsdp", None),
    )
    short = mesh.shape["fsdp"] == 8 and mesh.shape["group"] == 4
    return jax.shard_map(
        line if short else plain,
        mesh=mesh,
        in_specs=in_specs,
        out_specs=out_specs,
        check_vma=False,
    )
```

```python
import functools

import jax
import jax.numpy as jnp
from jax import lax
from jax.experimental import pallas as pl
from jax.experimental.pallas import tpu as pltpu
from jax.sharding import PartitionSpec as P

HEAD = 128
STEP = 100
CORR_ONE = 1.0 - 0.9**STEP
CORR_TWO = 1.0 - 0.95**STEP
PARTS = ((0, 256), (256, 256))
TILE = 256
BF16 = jnp.bfloat16
F32 = jnp.float32


def plain(
    activations,
    cotangent,
    inner_weights,
    first_moment,
    second_moment,
    anchor,
    outer_momentum,
    fragment,
):
    tokens_in = activations[0]
    upstream = cotangent[0]
    weights = inner_weights[0]
    low_weights = weights.astype(BF16)
    input_grad = lax.dot_general(
        upstream,
        lax.all_gather(low_weights, "fsdp", axis=0, tiled=True),
        (((1,), (1,)), ((), ())),
        preferred_element_type=F32,
    ).astype(BF16)
    gradient = lax.psum_scatter(
        lax.dot_general(tokens_in, upstream, (((0,), (0,)), ((), ())), preferred_element_type=F32),
        "fsdp",
        scatter_dimension=0,
        tiled=True,
    )
    new_first = 0.9 * first_moment[0] + 0.1 * gradient
    new_second = 0.95 * second_moment[0] + 0.05 * gradient * gradient
    update = new_first / CORR_ONE / (jnp.sqrt(new_second / CORR_TWO) + 1e-08) + 0.1 * weights
    stepped = weights - 0.1 * update
    offset = fragment[0] * HEAD
    local_cols = lax.dynamic_slice_in_dim(stepped, offset, HEAD, 1)
    anchor_cols = lax.dynamic_slice_in_dim(anchor, offset, HEAD, 1)
    moment_cols = lax.dynamic_slice_in_dim(outer_momentum, offset, HEAD, 1)
    summed = lax.psum((anchor_cols - local_cols).astype(BF16), "group").astype(F32)
    average = summed / lax.axis_size("group")
    moment_new = 0.9 * moment_cols + average
    anchor_next = anchor_cols - 0.7 * (average + 0.9 * moment_new)
    new_momentum = lax.dynamic_update_slice_in_dim(outer_momentum, moment_new, offset, 1)
    new_anchor = lax.dynamic_update_slice_in_dim(anchor, anchor_next, offset, 1)
    new_inner = lax.dynamic_update_slice_in_dim(stepped, anchor_next, offset, 1)
    return (
        input_grad[None],
        new_inner[None],
        new_first[None],
        new_second[None],
        new_anchor,
        new_momentum,
    )


def rows_by_columns(act, cot):
    return lax.dot_general(act, cot, (((0,), (0,)), ((), ())), preferred_element_type=F32)


def vmem(*shape, dtype=F32):
    return pltpu.VMEM(shape, dtype)


def hbm(*shape, dtype=F32):
    return jax.ShapeDtypeStruct(shape, dtype)


class Held:
    def __init__(self, array):
        self.array = array


def call(body, scalars, ins, outs, scratch=(), aliases=None, after=(), us=1.0):
    arrays, specs = [scalars], [pl.BlockSpec(memory_space=pltpu.SMEM)]
    for x in ins:
        if isinstance(x, Held):
            arrays.append(pltpu.with_memory_space_constraint(x.array, pltpu.VMEM))
            specs.append(pl.BlockSpec(memory_space=pltpu.VMEM))
        else:
            arrays.append(pltpu.with_memory_space_constraint(x, pltpu.HBM))
            specs.append(pl.BlockSpec(memory_space=pltpu.HBM))
    first = len(arrays)
    arrays += [pltpu.with_memory_space_constraint(x, pltpu.VMEM) for x in after]
    specs += [pl.BlockSpec(memory_space=pltpu.VMEM)] * len(after)

    def inner(*refs):
        body(*refs[:first], *refs[first + len(after) :])

    return pl.pallas_call(
        inner,
        in_specs=specs,
        out_specs=[
            pl.BlockSpec(memory_space=pl.ANY if isinstance(o, jax.ShapeDtypeStruct) else pltpu.VMEM)
            for o in outs
        ],
        out_shape=list(outs),
        scratch_shapes=list(scratch),
        input_output_aliases={1 + k: v for k, v in (aliases or {}).items()},
        cost_estimate=pl.CostEstimate(
            flops=0, bytes_accessed=int(us * 3.4e6), transcendentals=0
        ),
        compiler_params=pltpu.CompilerParams(vmem_limit_bytes=12 * 1024 * 1024),
    )(*arrays)


def columns_of(ref, block, width):
    return ref.at[:, pl.ds(pl.multiple_of(block * width, width), width)]


def start(src, dst, sem):
    copy = pltpu.make_async_copy(src, dst, sem)
    copy.start()
    return copy


def pieces(head):
    return (0, HEAD, head), (HEAD, HEAD, head ^ 1), (2 * HEAD, 2 * HEAD, 1 - head // 2)


def turned(at, s, src, dst, sems, base, first=0):
    return [
        start(
            columns_of(src, s[at["pieces"] + k], width),
            dst.at[:, pl.ds(column + first, width)],
            sems.at[base + k],
        )
        for k, (column, width, _) in enumerate(pieces(0))
    ]


def cast_body(offset, s, w, low, wide, sems):
    rows, part = low.shape
    step = rows // 2
    copies = [
        start(
            w.at[pl.ds(i * step, step), pl.ds(offset, part)],
            wide.at[pl.ds(i * step, step)],
            sems.at[i],
        )
        for i in range(2)
    ]
    for i, copy in enumerate(copies):
        copy.wait()

        @pl.loop(0, step // 64)
        def _(n):
            here = pl.ds(pl.multiple_of(i * step + n * 64, 64), 64)
            low[here, :] = wide[here, :].astype(BF16)


def load_blocks(at, s, act, cot, act_s, cot_v, sems):
    heads = turned(at, s, cot, cot_v, sems, 0)
    rows = act_s.shape[2]
    blocks = [
        start(columns_of(act, 2 * d + s[at["core"]], rows), act_s.at[d], sems.at[len(heads) + d])
        for d in range(act_s.shape[0])
    ]
    return heads, blocks


def own_body(at, s, act, cot, anchor, moment, *rest):
    sums_ref, anchor_out, moment_out, act_s, cot_v, held, sems = rest
    chips, _, rows = act_s.shape
    heads, blocks = load_blocks(at, s, act, cot, act_s, cot_v, sems)
    base = len(heads) + chips
    loads = [start(src, held.at[k], sems.at[base + k]) for k, src in enumerate((anchor, moment))]
    stores = []
    for k, dst in enumerate((anchor_out, moment_out)):
        loads[k].wait()
        stores.append(start(held.at[k], dst, sems.at[base + 2 + k]))
    for copy in heads + blocks:
        copy.wait()

    @pl.loop(0, chips)
    def _(d):
        for i in range(rows // TILE):
            here = pl.ds(pl.multiple_of(d * rows + i * TILE, TILE), TILE)
            sums_ref[here, :] = rows_by_columns(
                act_s[d, :, i * TILE : (i + 1) * TILE], cot_v[...]
            )

    for copy in stores:
        copy.wait()


def sibling_body(at, s, before, act, cot, w, m, v, anchor, moment, *rest):
    sums_ref, w_v, m_v, v_v, anchor_v, moment_v, act_s, cot_v, sems = rest
    chips, _, rows = act_s.shape
    heads, blocks = load_blocks(at, s, act, cot, act_s, cot_v, sems)
    base = len(heads) + chips
    copies = []
    for src, dst in ((w, w_v), (m, m_v), (v, v_v)):
        copies += turned(at, s, src, dst, sems, base + len(copies))
    for src, dst in ((anchor, anchor_v), (moment, moment_v)):
        copies.append(
            start(columns_of(src, s[at["pieces"]], HEAD), dst, sems.at[base + len(copies)])
        )
    for copy in heads + blocks:
        copy.wait()

    @pl.loop(0, chips)
    def _(d):
        for i in range(rows // TILE):
            here = pl.ds(pl.multiple_of(d * rows + i * TILE, TILE), TILE)
            sums_ref[here, :] = before[here, :] + rows_by_columns(
                act_s[d, :, i * TILE : (i + 1) * TILE], cot_v[...]
            )

    for copy in copies:
        copy.wait()


def hop_body(at, step, offset, s, sums_ref, from_o, from_e, *rest):
    to_e, to_o, picked = rest[-3:]
    older = rest[0] if step == 3 else None
    rows, part = to_e.shape
    columns = slice(offset, offset + part)
    base = at["hop"] + 4 * (step - 1)
    size = 64

    def each(body):
        @pl.loop(0, rows // size)
        def _(i):
            body(pl.multiple_of(i * size, size))

    for mode, block, src, dst in (
        (s[base], s[base + 1], from_o, to_e),
        (s[base + 2], s[base + 3], from_e, to_o),
    ):
        first = pl.multiple_of(block * rows, rows)

        @pl.when(mode == 0)
        def _():
            def body(r):
                dst[pl.ds(r, size), :] = sums_ref[pl.ds(first + r, size), columns].astype(BF16)

            each(body)

        @pl.when(mode == 1)
        def _():
            def body(r):
                here = pl.ds(r, size)
                added = src[here, :].astype(F32) + sums_ref[pl.ds(first + r, size), columns]
                dst[here, :] = added.astype(BF16)

            each(body)

        @pl.when(mode == 2)
        def _():
            def body(r):
                dst[pl.ds(r, size), :] = src[pl.ds(r, size), :]

            each(body)

    def keep(src):
        def body(r):
            picked[pl.ds(r, size), :] = src[pl.ds(r, size), :]

        each(body)

    if step == 1:
        keep(from_e)
    else:

        @pl.when(s[at["middle"]] == 1)
        def _():
            keep(from_o if older is None else older)

        @pl.when(s[at["middle"]] == 0)
        def _():
            keep(from_e)


def grad_body(at, which, s, cot_own, cot_sib, *rest):
    theirs, out, token, stage, sems = rest[-5:]
    rows = stage.shape[1]
    copies = []
    if which > 0:
        copies.append(
            start(
                rest[len(PARTS)], columns_of(out, s[at["grad"] + 2 * which - 1], rows), sems.at[1]
            )
        )
    for cot, dst in ((cot_sib, theirs), (cot_own, stage)):
        for i in range(rows // TILE):
            here = slice(i * TILE, (i + 1) * TILE)
            total = None
            for (offset, part), block in zip(PARTS, rest):
                term = lax.dot_general(
                    cot[:, offset : offset + part],
                    block[here, :],
                    (((1,), (1,)), ((), ())),
                    preferred_element_type=F32,
                )
                total = term if total is None else total + term
            dst[:, here] = total.astype(BF16)
    copies.append(start(stage, columns_of(out, s[at["grad"] + 2 * which], rows), sems.at[0]))
    token[...] = jnp.zeros_like(token)
    for copy in copies:
        copy.wait()


def adam(at, offset, first_row, s, sums_ref, from_e, from_o, w, m, v, put, count, width, taken):
    columns = slice(offset, offset + width)
    size = 128
    base = pl.multiple_of(s[at["z"]] * from_e.shape[0], TILE)

    @pl.loop(0, count // size)
    def _(i):
        r = pl.multiple_of(first_row + i * size, size)
        here = pl.ds(r, size)
        one = sums_ref[pl.ds(base + r, size), columns] + from_e[here, taken].astype(F32)
        both = one + from_o[here, taken].astype(F32)
        gradient = jnp.where(s[at["middle"]] == 1, both, one)
        first = 0.9 * m[here, columns] + 0.1 * gradient
        second = 0.95 * v[here, columns] + 0.05 * gradient * gradient
        scaled = second * (1.0 / CORR_TWO)
        below = scaled * lax.rsqrt(scaled) + 1e-08
        over = pl.reciprocal(below, approx=True)
        over = over * (2.0 - below * over)
        stepped = (1.0 - 0.1 * 0.1) * w[here, columns] - first * (0.1 / CORR_ONE) * over
        put(r, stepped, first, second)


def head_body(at, s, sums_ref, from_e, from_o, w, m, v, anchor, upper, lower, first_v, second_v):
    rows = anchor.shape[0]
    for k, diff in enumerate((upper, lower)):
        top = k * rows // 2

        def put(r, stepped, first, second):
            here = pl.ds(r, stepped.shape[0])
            first_v[here, :] = first
            second_v[here, :] = second
            there = pl.ds(r - top, stepped.shape[0])
            diff[there, :] = (anchor[here, :] - stepped).astype(BF16)

        args = (from_e, from_o, w, m, v, put, rows // 2, HEAD, slice(0, HEAD))
        adam(at, 0, top, s, sums_ref, *args)


def rest_body(at, offset, part, within, s, sums_ref, from_e, from_o, w, m, v, *rest):
    stage, sems = rest[-2:]
    rows = from_e.shape[0]
    tiles = rows // TILE
    copies = []
    if within:
        first_v, second_v, theirs = rest[:3]
        *outs, grads, token = rest[4:-2]
        for k, src in enumerate((first_v, second_v)):
            there = columns_of(outs[1 + k], s[at["pieces"]], HEAD)
            copies.append(start(src, there, sems.at[k]))
        copies.append(start(theirs, columns_of(grads, s[at["grad"] + 7], rows), sems.at[2]))
        token[...] = jnp.zeros_like(token)
    else:
        tiles -= 1
        *outs, left = rest[3:-2]
    piece = next(k for k, (column, *_) in enumerate(pieces(0)) if column == offset)
    args = (from_e, from_o, w, m, v)
    taken = slice(within, within + part)

    def putter(refs, top):
        def put(r, *values):
            here = pl.ds(r - top, values[0].shape[0])
            for k, value in enumerate(values):
                refs[k, here, :] = value

        return put

    for tile in range(tiles):
        first = tile * TILE
        adam(at, offset, first, s, sums_ref, *args, putter(stage, 0), TILE, part, taken)
        there = pl.ds(first, TILE)
        for k, out in enumerate(outs):
            copies.append(
                start(
                    stage.at[k, there],
                    columns_of(out.at[there], s[at["pieces"] + piece], part),
                    sems.at[len(copies)],
                )
            )
    if not within:
        first = tiles * TILE
        adam(at, offset, first, s, sums_ref, *args, putter(left, first), TILE, part, taken)
    for copy in copies:
        copy.wait()


def mix(own, other, token):
    return (own.astype(F32) + other.astype(F32) + token[:1]).astype(BF16)


def outer_body(at, s, left, upper, upper_in, lower, lower_in, anchor, moment, *rest):
    inner, first, second, new_anchor, new_moment, stage, sems = rest[5:]
    rows = anchor.shape[0]
    _, count, part = left.shape
    there = pl.ds(rows - count, count)
    copies = []
    for k, out in enumerate((inner, first, second)):
        last = columns_of(out.at[there], s[at["pieces"] + 2], part)
        copies.append(start(left.at[k], last, sems.at[k]))
    half = rows // 2
    size = 128
    for n, (own, other) in enumerate(((upper, upper_in), (lower, lower_in))):

        @pl.loop(0, half // size)
        def _(i):
            r = pl.multiple_of(i * size, size)
            here, there = pl.ds(r, size), pl.ds(n * half + r, size)
            average = (own[here, :].astype(F32) + other[here, :].astype(F32)) / 4.0
            momentum = 0.9 * moment[there, :] + average
            stage[0, there, :] = momentum
            stage[1, there, :] = anchor[there, :] - 0.7 * (average + 0.9 * momentum)

    for k, out in ((0, new_moment), (1, new_anchor), (1, inner)):
        columns = columns_of(out, s[at["pieces"]], HEAD)
        copies.append(start(stage.at[k], columns, sems.at[len(copies)]))
    for copy in copies:
        copy.wait()


def line(
    activations,
    cotangent,
    inner_weights,
    first_moment,
    second_moment,
    anchor,
    outer_momentum,
    fragment,
):
    act, cot, weights = activations[0], cotangent[0], inner_weights[0]
    moment, second = first_moment[0], second_moment[0]
    tokens, width = act.shape
    rows, columns = weights.shape
    chips = lax.axis_size("fsdp") // 2
    me = lax.axis_index("fsdp")
    z, core = me // 2, me % 2
    head = fragment[0]
    last = chips - 1
    middle = (z > 0) & (z < last)
    even = z % 2 == 0
    zd = last - z

    def cross(i):
        return i ^ 1 if i // 2 in (0, last) else (i + 2 if i // 2 % 2 else i - 2)

    e_perm = [(i, i ^ 2) for i in range(2 * chips)]
    o_perm = [(i, cross(i)) for i in range(2 * chips)]
    swap = [(i, i ^ 1) for i in range(2 * chips)]
    x_perm, y_perm = [(i, i ^ 1) for i in range(4)], [(i, i ^ 2) for i in range(4)]

    values, at = [], {}

    def name(key, *numbers):
        at[key] = len(values)
        values.extend(jnp.asarray(v, jnp.int32) for v in numbers)

    name("z", z)
    name("core", core)
    name("middle", middle)
    name("pieces", *[block for _, _, block in pieces(head)])
    name("grad", *[2 * (z ^ k) + c for k in range(chips) for c in (core, 1 - core)])
    hops = []
    for step in range(1, chips):
        up_mode = jnp.where(step <= z, 2, jnp.where(z == 0, 0, 1))
        down_mode = jnp.where(step <= zd, 2, jnp.where(zd == 0, 0, 1))
        up_to = jnp.clip(chips - step + z, 0, last)
        down_to = jnp.clip(step - 1 - zd, 0, last)
        hops += [
            jnp.where(even, up_mode, down_mode),
            jnp.where(even, up_to, down_to),
            jnp.where(middle, jnp.where(even, down_mode, up_mode), 2),
            jnp.where(even, down_to, up_to),
        ]
    name("hop", *hops)
    s = jnp.stack(values)

    def permute(x, perm, axis="fsdp"):
        return lax.ppermute(x, axis, perm)

    dma = pltpu.SemaphoreType.DMA
    from_e, from_o = [[]], [[]]
    act_sib, cot_sib = permute(act, swap), permute(cot, swap)
    (_, first), (offset, part) = PARTS
    low = [weights[:, :first].astype(BF16)]
    low += call(
        functools.partial(cast_body, offset),
        s,
        [weights],
        [vmem(rows, part, dtype=BF16)],
        [vmem(rows, part), dma((2,))],
        after=[cot_sib],
        us=2.0,
    )
    for x in low:
        from_e[0].append(permute(x, e_perm))
        from_o[0].append(permute(x, o_perm))

    sums_shape = vmem(chips * rows, columns)
    cot_shape = vmem(tokens, columns, dtype=BF16)
    block_shape = vmem(chips, tokens, rows, dtype=BF16)
    sums_own, new_anchor, new_momentum = call(
        functools.partial(own_body, at),
        s,
        [act, Held(cot), anchor, outer_momentum],
        [sums_shape, hbm(rows, columns), hbm(rows, columns)],
        [block_shape, cot_shape, vmem(2, rows, columns), dma((chips + 7,))],
        after=low[-1:],
        us=5.0,
    )
    sums_both, w_v, m_v, v_v, anchor_v, moment_v = call(
        functools.partial(sibling_body, at),
        s,
        [Held(sums_own), act_sib, Held(cot_sib), weights, moment, second, anchor, outer_momentum],
        [sums_shape] + [vmem(rows, columns)] * 3 + [vmem(rows, HEAD)] * 2,
        [block_shape, cot_shape, dma((chips + 14,))],
        {0: 0},
        us=5.0,
    )

    def hop(step, j, after):
        offset, part = PARTS[j]
        ins = [Held(sums_both), Held(from_o[step - 1][j]), Held(from_e[step - 1][j])]
        if step == 3:
            ins += [Held(from_o[0][j])]
        return call(
            functools.partial(hop_body, at, step, offset),
            s,
            ins,
            [vmem(rows, part, dtype=BF16)] * 3,
            after=after,
        )

    def grad(which, before, own, after):
        ins = [Held(x) for x in [cot, cot_sib, *own]]
        aliases = {}
        if before is not None:
            theirs, buffer = before
            ins += [Held(theirs)]
            aliases = {len(ins): 1}
            ins += [buffer]
        theirs, buffer, token = call(
            functools.partial(grad_body, at, which),
            s,
            ins,
            [
                vmem(tokens, rows, dtype=BF16),
                hbm(tokens, width, dtype=BF16),
                vmem(8, 128),
            ],
            [vmem(tokens, rows, dtype=BF16), dma((2,))],
            aliases,
            after,
            us=2.1,
        )
        return (permute(theirs, swap), buffer), token

    grads, after, picked = None, (), low
    for step in range(1, chips):
        from_e.append([])
        from_o.append([])
        found = []
        for j in range(len(PARTS)):
            to_e, to_o, pick = hop(step, j, after)
            from_e[step].append(permute(to_e, e_perm))
            from_o[step].append(permute(to_o, o_perm))
            found.append(pick)
            after = ()
            if j == 0:
                grads, token = grad(step - 1, grads, picked, (to_e,))
                after = (token,)
        picked = found
    grads, token = grad(last, grads, picked, ())

    theirs, input_grad = grads
    half = vmem(rows // 2, HEAD, dtype=BF16)
    full = [hbm(rows, columns)] * 3

    def inputs(j):
        return [sums_both, from_e[last][j], from_o[last][j], w_v, m_v, v_v]

    upper, lower, first_v, second_v = call(
        functools.partial(head_body, at),
        s,
        [Held(x) for x in [*inputs(0), anchor_v]],
        [half, half, vmem(rows, HEAD), vmem(rows, HEAD)],
        after=(token,),
        us=1.0,
    )
    upper_in = permute(upper, x_perm, "group")
    lower_in = permute(lower, y_perm, "group")
    *state, input_grad, token = call(
        functools.partial(rest_body, at, HEAD, PARTS[0][1] - HEAD, HEAD),
        s,
        [Held(x) for x in [*inputs(0), first_v, second_v, theirs]] + [input_grad],
        full + [hbm(tokens, width, dtype=BF16), vmem(8, 128)],
        [vmem(3, rows, PARTS[0][1] - HEAD), dma((3 + 3 * rows // TILE,))],
        {9: 3},
        us=2.0,
    )
    upper, lower = mix(upper, upper_in, token), mix(lower, lower_in, token)
    upper_in = permute(upper, y_perm, "group")
    lower_in = permute(lower, x_perm, "group")
    offset, part = PARTS[1]
    *state, left = call(
        functools.partial(rest_body, at, offset, part, 0),
        s,
        [Held(x) for x in inputs(1)] + state,
        full + [vmem(3, TILE, part)],
        [vmem(3, rows, part), dma((3 * rows // TILE,))],
        {6: 0, 7: 1, 8: 2},
        after=(upper, lower),
        us=2.4,
    )
    held = [left, upper, upper_in, lower, lower_in, anchor_v, moment_v]
    inner, new_first, new_second, new_anchor, new_momentum = call(
        functools.partial(outer_body, at),
        s,
        [Held(x) for x in held] + [*state, new_anchor, new_momentum],
        [hbm(rows, columns)] * 5,
        [vmem(2, rows, HEAD), dma((6,))],
        {len(held) + k: k for k in range(5)},
        us=2.0,
    )
    return (
        input_grad[None],
        inner[None],
        new_first[None],
        new_second[None],
        new_anchor,
        new_momentum,
    )


def solution(mesh):
    in_specs = (
        P("group", "fsdp", None),
        P("group", "fsdp", None),
        P("group", "fsdp", None),
        P("group", "fsdp", None),
        P("group", "fsdp", None),
        P("fsdp", None),
        P("fsdp", None),
        P(),
    )
    out_specs = (
        P("group", "fsdp", None),
        P("group", "fsdp", None),
        P("group", "fsdp", None),
        P("group", "fsdp", None),
        P("fsdp", None),
        P("fsdp", None),
    )
    short = mesh.shape["fsdp"] == 8 and mesh.shape["group"] == 4
    return jax.shard_map(
        line if short else plain,
        mesh=mesh,
        in_specs=in_specs,
        out_specs=out_specs,
        check_vma=False,
    )
```

```python
import functools

import jax
import jax.numpy as jnp
from jax import lax
from jax.experimental import pallas as pl
from jax.experimental.pallas import tpu as pltpu
from jax.sharding import PartitionSpec as P

HEAD = 128
STEP = 100
CORR_ONE = 1.0 - 0.9**STEP
CORR_TWO = 1.0 - 0.95**STEP
PARTS = ((0, 256), (256, 256))
TILE = 256
BF16 = jnp.bfloat16
F32 = jnp.float32


def plain(
    activations,
    cotangent,
    inner_weights,
    first_moment,
    second_moment,
    anchor,
    outer_momentum,
    fragment,
):
    tokens_in = activations[0]
    upstream = cotangent[0]
    weights = inner_weights[0]
    low_weights = weights.astype(BF16)
    input_grad = lax.dot_general(
        upstream,
        lax.all_gather(low_weights, "fsdp", axis=0, tiled=True),
        (((1,), (1,)), ((), ())),
        preferred_element_type=F32,
    ).astype(BF16)
    gradient = lax.psum_scatter(
        lax.dot_general(tokens_in, upstream, (((0,), (0,)), ((), ())), preferred_element_type=F32),
        "fsdp",
        scatter_dimension=0,
        tiled=True,
    )
    new_first = 0.9 * first_moment[0] + 0.1 * gradient
    new_second = 0.95 * second_moment[0] + 0.05 * gradient * gradient
    update = new_first / CORR_ONE / (jnp.sqrt(new_second / CORR_TWO) + 1e-08) + 0.1 * weights
    stepped = weights - 0.1 * update
    offset = fragment[0] * HEAD
    local_cols = lax.dynamic_slice_in_dim(stepped, offset, HEAD, 1)
    anchor_cols = lax.dynamic_slice_in_dim(anchor, offset, HEAD, 1)
    moment_cols = lax.dynamic_slice_in_dim(outer_momentum, offset, HEAD, 1)
    summed = lax.psum((anchor_cols - local_cols).astype(BF16), "group").astype(F32)
    average = summed / lax.axis_size("group")
    moment_new = 0.9 * moment_cols + average
    anchor_next = anchor_cols - 0.7 * (average + 0.9 * moment_new)
    new_momentum = lax.dynamic_update_slice_in_dim(outer_momentum, moment_new, offset, 1)
    new_anchor = lax.dynamic_update_slice_in_dim(anchor, anchor_next, offset, 1)
    new_inner = lax.dynamic_update_slice_in_dim(stepped, anchor_next, offset, 1)
    return (
        input_grad[None],
        new_inner[None],
        new_first[None],
        new_second[None],
        new_anchor,
        new_momentum,
    )


def rows_by_columns(act, cot):
    return lax.dot_general(act, cot, (((0,), (0,)), ((), ())), preferred_element_type=F32)


def vmem(*shape, dtype=F32):
    return pltpu.VMEM(shape, dtype)


def hbm(*shape, dtype=F32):
    return jax.ShapeDtypeStruct(shape, dtype)


class Numbers:
    def __init__(self, ref):
        self.ref, self.read = ref, {}

    def __getitem__(self, k):
        if k not in self.read:
            self.read[k] = self.ref[0, k]
        return self.read[k]


class Held:
    def __init__(self, array):
        self.array = array


def call(body, scalars, ins, outs, scratch=(), aliases=None, after=(), us=1.0):
    arrays, specs = [], []
    for x in [Held(scalars), *ins]:
        if isinstance(x, Held):
            arrays.append(pltpu.with_memory_space_constraint(x.array, pltpu.VMEM))
            specs.append(pl.BlockSpec(memory_space=pltpu.VMEM))
        else:
            arrays.append(pltpu.with_memory_space_constraint(x, pltpu.HBM))
            specs.append(pl.BlockSpec(memory_space=pltpu.HBM))
    first = len(arrays)
    arrays += [pltpu.with_memory_space_constraint(x, pltpu.VMEM) for x in after]
    specs += [pl.BlockSpec(memory_space=pltpu.VMEM)] * len(after)

    def inner(*refs):
        body(Numbers(refs[0]), *refs[1:first], *refs[first + len(after) :])

    return pl.pallas_call(
        inner,
        in_specs=specs,
        out_specs=[
            pl.BlockSpec(memory_space=pl.ANY if isinstance(o, jax.ShapeDtypeStruct) else pltpu.VMEM)
            for o in outs
        ],
        out_shape=list(outs),
        scratch_shapes=list(scratch),
        input_output_aliases={1 + k: v for k, v in (aliases or {}).items()},
        cost_estimate=pl.CostEstimate(
            flops=0, bytes_accessed=int(us * 3.4e6), transcendentals=0
        ),
        compiler_params=pltpu.CompilerParams(vmem_limit_bytes=12 * 1024 * 1024),
    )(*arrays)


def columns_of(ref, block, width):
    return ref.at[:, pl.ds(pl.multiple_of(block * width, width), width)]


def start(src, dst, sem):
    copy = pltpu.make_async_copy(src, dst, sem)
    copy.start()
    return copy


def pieces(head):
    return (0, HEAD, head), (HEAD, HEAD, head ^ 1), (2 * HEAD, 2 * HEAD, 1 - head // 2)


def turned(at, s, src, dst, sems, base, first=0):
    return [
        start(
            columns_of(src, s[at["pieces"] + k], width),
            dst.at[:, pl.ds(column + first, width)],
            sems.at[base + k],
        )
        for k, (column, width, _) in enumerate(pieces(0))
    ]


def cast_body(offset, s, w, low, wide, sems):
    rows, part = low.shape
    step = rows // 2
    copies = [
        start(
            w.at[pl.ds(i * step, step), pl.ds(offset, part)],
            wide.at[pl.ds(i * step, step)],
            sems.at[i],
        )
        for i in range(2)
    ]
    for i, copy in enumerate(copies):
        copy.wait()

        @pl.loop(0, step // 64)
        def _(n):
            here = pl.ds(pl.multiple_of(i * step + n * 64, 64), 64)
            low[here, :] = wide[here, :].astype(BF16)


def load_blocks(at, s, act, cot, act_s, cot_v, sems):
    heads = turned(at, s, cot, cot_v, sems, 0)
    rows = act_s.shape[2]
    blocks = [
        start(columns_of(act, 2 * d + s[at["core"]], rows), act_s.at[d], sems.at[len(heads) + d])
        for d in range(act_s.shape[0])
    ]
    return heads, blocks


def own_body(at, s, act, cot, anchor, moment, *rest):
    sums_ref, anchor_out, moment_out, act_s, cot_v, held, sems = rest
    chips, _, rows = act_s.shape
    heads, blocks = load_blocks(at, s, act, cot, act_s, cot_v, sems)
    base = len(heads) + chips
    loads = [start(src, held.at[k], sems.at[base + k]) for k, src in enumerate((anchor, moment))]
    stores = []
    for k, dst in enumerate((anchor_out, moment_out)):
        loads[k].wait()
        stores.append(start(held.at[k], dst, sems.at[base + 2 + k]))
    for copy in heads + blocks:
        copy.wait()

    @pl.loop(0, chips)
    def _(d):
        for i in range(rows // TILE):
            here = pl.ds(pl.multiple_of(d * rows + i * TILE, TILE), TILE)
            sums_ref[here, :] = rows_by_columns(
                act_s[d, :, i * TILE : (i + 1) * TILE], cot_v[...]
            )

    for copy in stores:
        copy.wait()


def sibling_body(at, s, before, act, cot, w, m, v, anchor, moment, *rest):
    sums_ref, w_v, m_v, v_v, anchor_v, moment_v, act_s, cot_v, sems = rest
    chips, _, rows = act_s.shape
    heads, blocks = load_blocks(at, s, act, cot, act_s, cot_v, sems)
    base = len(heads) + chips
    copies = []
    for src, dst in ((w, w_v), (m, m_v), (v, v_v)):
        copies += turned(at, s, src, dst, sems, base + len(copies))
    for src, dst in ((anchor, anchor_v), (moment, moment_v)):
        copies.append(
            start(columns_of(src, s[at["pieces"]], HEAD), dst, sems.at[base + len(copies)])
        )
    for copy in heads + blocks:
        copy.wait()

    @pl.loop(0, chips)
    def _(d):
        for i in range(rows // TILE):
            here = pl.ds(pl.multiple_of(d * rows + i * TILE, TILE), TILE)
            sums_ref[here, :] = before[here, :] + rows_by_columns(
                act_s[d, :, i * TILE : (i + 1) * TILE], cot_v[...]
            )

    for copy in copies:
        copy.wait()


def hop_body(at, step, offset, s, sums_ref, from_o, from_e, *rest):
    to_e, to_o, picked = rest[-3:]
    older = rest[0] if step == 3 else None
    rows, part = to_e.shape
    columns = slice(offset, offset + part)
    base = at["hop"] + 4 * (step - 1)
    size = 64

    def each(body):
        @pl.loop(0, rows // size)
        def _(i):
            body(pl.multiple_of(i * size, size))

    for mode, block, src, dst in (
        (s[base], s[base + 1], from_o, to_e),
        (s[base + 2], s[base + 3], from_e, to_o),
    ):
        first = pl.multiple_of(block * rows, rows)

        @pl.when(mode == 0)
        def _():
            def body(r):
                dst[pl.ds(r, size), :] = sums_ref[pl.ds(first + r, size), columns].astype(BF16)

            each(body)

        @pl.when(mode == 1)
        def _():
            def body(r):
                here = pl.ds(r, size)
                added = src[here, :].astype(F32) + sums_ref[pl.ds(first + r, size), columns]
                dst[here, :] = added.astype(BF16)

            each(body)

        @pl.when(mode == 2)
        def _():
            def body(r):
                dst[pl.ds(r, size), :] = src[pl.ds(r, size), :]

            each(body)

    def keep(src):
        def body(r):
            picked[pl.ds(r, size), :] = src[pl.ds(r, size), :]

        each(body)

    if step == 1:
        keep(from_e)
    else:

        @pl.when(s[at["middle"]] == 1)
        def _():
            keep(from_o if older is None else older)

        @pl.when(s[at["middle"]] == 0)
        def _():
            keep(from_e)


def grad_body(at, which, s, cot_own, cot_sib, *rest):
    theirs, out, token, stage, sems = rest[-5:]
    rows = stage.shape[1]
    copies = []
    if which > 0:
        copies.append(
            start(
                rest[len(PARTS)], columns_of(out, s[at["grad"] + 2 * which - 1], rows), sems.at[1]
            )
        )
    for cot, dst in ((cot_sib, theirs), (cot_own, stage)):
        for i in range(rows // TILE):
            here = slice(i * TILE, (i + 1) * TILE)
            total = None
            for (offset, part), block in zip(PARTS, rest):
                term = lax.dot_general(
                    cot[:, offset : offset + part],
                    block[here, :],
                    (((1,), (1,)), ((), ())),
                    preferred_element_type=F32,
                )
                total = term if total is None else total + term
            dst[:, here] = total.astype(BF16)
    copies.append(start(stage, columns_of(out, s[at["grad"] + 2 * which], rows), sems.at[0]))
    token[...] = jnp.zeros_like(token)
    for copy in copies:
        copy.wait()


def adam(at, offset, first_row, s, sums_ref, from_e, from_o, w, m, v, put, count, width, taken):
    columns = slice(offset, offset + width)
    size = 256
    base = pl.multiple_of(s[at["z"]] * from_e.shape[0], TILE)
    middle = s[at["middle"]] == 1

    @pl.loop(0, count // size)
    def _(i):
        r = pl.multiple_of(first_row + i * size, size)
        here = pl.ds(r, size)
        one = sums_ref[pl.ds(base + r, size), columns] + from_e[here, taken].astype(F32)
        both = one + from_o[here, taken].astype(F32)
        gradient = jnp.where(middle, both, one)
        first = 0.9 * m[here, columns] + 0.1 * gradient
        second = 0.95 * v[here, columns] + 0.05 * gradient * gradient
        below = second * lax.rsqrt(second) + 1e-08 * CORR_TWO**0.5
        moved = first * (0.1 * CORR_TWO**0.5 / CORR_ONE) / below
        stepped = (1.0 - 0.1 * 0.1) * w[here, columns] - moved
        put(r, stepped, first, second)


def head_body(at, s, sums_ref, from_e, from_o, w, m, v, anchor, upper, lower, first_v, second_v):
    rows = anchor.shape[0]
    for k, diff in enumerate((upper, lower)):
        top = k * rows // 2

        def put(r, stepped, first, second):
            here = pl.ds(r, stepped.shape[0])
            first_v[here, :] = first
            second_v[here, :] = second
            there = pl.ds(r - top, stepped.shape[0])
            diff[there, :] = (anchor[here, :] - stepped).astype(BF16)

        args = (from_e, from_o, w, m, v, put, rows // 2, HEAD, slice(0, HEAD))
        adam(at, 0, top, s, sums_ref, *args)


def rest_body(at, offset, part, within, s, sums_ref, from_e, from_o, w, m, v, *rest):
    stage, sems = rest[-2:]
    rows = from_e.shape[0]
    tiles = rows // TILE
    copies = []
    if within:
        first_v, second_v, theirs = rest[:3]
        *outs, grads, token = rest[4:-2]
        for k, src in enumerate((first_v, second_v)):
            there = columns_of(outs[1 + k], s[at["pieces"]], HEAD)
            copies.append(start(src, there, sems.at[k]))
        copies.append(start(theirs, columns_of(grads, s[at["grad"] + 7], rows), sems.at[2]))
        token[...] = jnp.zeros_like(token)
    else:
        tiles -= 1
        *outs, left = rest[3:-2]
    piece = next(k for k, (column, *_) in enumerate(pieces(0)) if column == offset)
    args = (from_e, from_o, w, m, v)
    taken = slice(within, within + part)

    def putter(refs, top):
        def put(r, *values):
            here = pl.ds(r - top, values[0].shape[0])
            for k, value in enumerate(values):
                refs[k, here, :] = value

        return put

    for tile in range(tiles):
        first = tile * TILE
        adam(at, offset, first, s, sums_ref, *args, putter(stage, 0), TILE, part, taken)
        there = pl.ds(first, TILE)
        for k, out in enumerate(outs):
            copies.append(
                start(
                    stage.at[k, there],
                    columns_of(out.at[there], s[at["pieces"] + piece], part),
                    sems.at[len(copies)],
                )
            )
    if not within:
        first = tiles * TILE
        adam(at, offset, first, s, sums_ref, *args, putter(left, first), TILE, part, taken)
    for copy in copies:
        copy.wait()


def mix(own, other, token):
    return (own.astype(F32) + other.astype(F32) + token[:1]).astype(BF16)


def outer_body(at, s, left, upper, upper_in, lower, lower_in, anchor, moment, *rest):
    inner, first, second, new_anchor, new_moment, stage, sems = rest[5:]
    rows = anchor.shape[0]
    _, count, part = left.shape
    there = pl.ds(rows - count, count)
    copies = []
    for k, out in enumerate((inner, first, second)):
        last = columns_of(out.at[there], s[at["pieces"] + 2], part)
        copies.append(start(left.at[k], last, sems.at[k]))
    half = rows // 2
    size = half // 2
    for n, (own, other) in enumerate(((upper, upper_in), (lower, lower_in))):
        for r in (0, size):
            here, there = pl.ds(r, size), pl.ds(n * half + r, size)
            average = (own[here, :].astype(F32) + other[here, :].astype(F32)) * 0.25
            momentum = 0.9 * moment[there, :] + average
            stage[0, there, :] = momentum
            stage[1, there, :] = anchor[there, :] - 0.7 * (average + 0.9 * momentum)
            for k, out in ((0, new_moment), (1, new_anchor), (1, inner)):
                target = columns_of(out.at[there], s[at["pieces"]], HEAD)
                copies.append(start(stage.at[k, there], target, sems.at[len(copies)]))
    for copy in copies:
        copy.wait()


def line(
    activations,
    cotangent,
    inner_weights,
    first_moment,
    second_moment,
    anchor,
    outer_momentum,
    fragment,
):
    act, cot, weights = activations[0], cotangent[0], inner_weights[0]
    moment, second = first_moment[0], second_moment[0]
    tokens, width = act.shape
    rows, columns = weights.shape
    chips = lax.axis_size("fsdp") // 2
    me = lax.axis_index("fsdp")
    z, core = me // 2, me % 2
    head = fragment[0]
    last = chips - 1
    middle = (z > 0) & (z < last)
    even = z % 2 == 0
    zd = last - z

    def cross(i):
        return i ^ 1 if i // 2 in (0, last) else (i + 2 if i // 2 % 2 else i - 2)

    e_perm = [(i, i ^ 2) for i in range(2 * chips)]
    o_perm = [(i, cross(i)) for i in range(2 * chips)]
    swap = [(i, i ^ 1) for i in range(2 * chips)]
    x_perm, y_perm = [(i, i ^ 1) for i in range(4)], [(i, i ^ 2) for i in range(4)]

    values, at = [], {}

    def name(key, *numbers):
        at[key] = len(values)
        values.extend(jnp.asarray(v, jnp.int32) for v in numbers)

    name("z", z)
    name("core", core)
    name("middle", middle)
    name("pieces", *[block for _, _, block in pieces(head)])
    name("grad", *[2 * (z ^ k) + c for k in range(chips) for c in (core, 1 - core)])
    hops = []
    for step in range(1, chips):
        up_mode = jnp.where(step <= z, 2, jnp.where(z == 0, 0, 1))
        down_mode = jnp.where(step <= zd, 2, jnp.where(zd == 0, 0, 1))
        up_to = jnp.clip(chips - step + z, 0, last)
        down_to = jnp.clip(step - 1 - zd, 0, last)
        hops += [
            jnp.where(even, up_mode, down_mode),
            jnp.where(even, up_to, down_to),
            jnp.where(middle, jnp.where(even, down_mode, up_mode), 2),
            jnp.where(even, down_to, up_to),
        ]
    name("hop", *hops)
    s = jnp.pad(jnp.stack(values), (0, 128 - len(values)))[None]

    def permute(x, perm, axis="fsdp"):
        return lax.ppermute(x, axis, perm)

    dma = pltpu.SemaphoreType.DMA
    from_e, from_o = [[]], [[]]
    act_sib, cot_sib = permute(act, swap), permute(cot, swap)
    (_, first), (offset, part) = PARTS
    low = [weights[:, :first].astype(BF16)]
    low += call(
        functools.partial(cast_body, offset),
        s,
        [weights],
        [vmem(rows, part, dtype=BF16)],
        [vmem(rows, part), dma((2,))],
        after=[cot_sib],
        us=2.0,
    )
    for x in low:
        from_e[0].append(permute(x, e_perm))
        from_o[0].append(permute(x, o_perm))

    sums_shape = vmem(chips * rows, columns)
    cot_shape = vmem(tokens, columns, dtype=BF16)
    block_shape = vmem(chips, tokens, rows, dtype=BF16)
    sums_own, new_anchor, new_momentum = call(
        functools.partial(own_body, at),
        s,
        [act, Held(cot), anchor, outer_momentum],
        [sums_shape, hbm(rows, columns), hbm(rows, columns)],
        [block_shape, cot_shape, vmem(2, rows, columns), dma((chips + 7,))],
        after=low[-1:],
        us=5.0,
    )
    sums_both, w_v, m_v, v_v, anchor_v, moment_v = call(
        functools.partial(sibling_body, at),
        s,
        [Held(sums_own), act_sib, Held(cot_sib), weights, moment, second, anchor, outer_momentum],
        [sums_shape] + [vmem(rows, columns)] * 3 + [vmem(rows, HEAD)] * 2,
        [block_shape, cot_shape, dma((chips + 14,))],
        {0: 0},
        us=5.0,
    )

    def hop(step, j, after):
        offset, part = PARTS[j]
        ins = [Held(sums_both), Held(from_o[step - 1][j]), Held(from_e[step - 1][j])]
        if step == 3:
            ins += [Held(from_o[0][j])]
        return call(
            functools.partial(hop_body, at, step, offset),
            s,
            ins,
            [vmem(rows, part, dtype=BF16)] * 3,
            after=after,
        )

    def grad(which, before, own, after):
        ins = [Held(x) for x in [cot, cot_sib, *own]]
        aliases = {}
        if before is not None:
            theirs, buffer = before
            ins += [Held(theirs)]
            aliases = {len(ins): 1}
            ins += [buffer]
        theirs, buffer, token = call(
            functools.partial(grad_body, at, which),
            s,
            ins,
            [
                vmem(tokens, rows, dtype=BF16),
                hbm(tokens, width, dtype=BF16),
                vmem(8, 128),
            ],
            [vmem(tokens, rows, dtype=BF16), dma((2,))],
            aliases,
            after,
            us=2.1,
        )
        return (permute(theirs, swap), buffer), token

    grads, after, picked = None, (), low
    for step in range(1, chips):
        from_e.append([])
        from_o.append([])
        found = []
        for j in range(len(PARTS)):
            to_e, to_o, pick = hop(step, j, after)
            from_e[step].append(permute(to_e, e_perm))
            from_o[step].append(permute(to_o, o_perm))
            found.append(pick)
            after = ()
            if j == 0:
                grads, token = grad(step - 1, grads, picked, (to_e,))
                after = (token,)
        picked = found
    grads, token = grad(last, grads, picked, ())

    theirs, input_grad = grads
    half = vmem(rows // 2, HEAD, dtype=BF16)
    full = [hbm(rows, columns)] * 3

    def inputs(j):
        return [sums_both, from_e[last][j], from_o[last][j], w_v, m_v, v_v]

    upper, lower, first_v, second_v = call(
        functools.partial(head_body, at),
        s,
        [Held(x) for x in [*inputs(0), anchor_v]],
        [half, half, vmem(rows, HEAD), vmem(rows, HEAD)],
        after=(token,),
        us=1.0,
    )
    upper_in = permute(upper, x_perm, "group")
    lower_in = permute(lower, y_perm, "group")
    *state, input_grad, token = call(
        functools.partial(rest_body, at, HEAD, PARTS[0][1] - HEAD, HEAD),
        s,
        [Held(x) for x in [*inputs(0), first_v, second_v, theirs]] + [input_grad],
        full + [hbm(tokens, width, dtype=BF16), vmem(8, 128)],
        [vmem(3, rows, PARTS[0][1] - HEAD), dma((3 + 3 * rows // TILE,))],
        {9: 3},
        us=2.0,
    )
    upper, lower = mix(upper, upper_in, token), mix(lower, lower_in, token)
    upper_in = permute(upper, y_perm, "group")
    lower_in = permute(lower, x_perm, "group")
    offset, part = PARTS[1]
    *state, left = call(
        functools.partial(rest_body, at, offset, part, 0),
        s,
        [Held(x) for x in inputs(1)] + state,
        full + [vmem(3, TILE, part)],
        [vmem(3, rows, part), dma((3 * rows // TILE,))],
        {6: 0, 7: 1, 8: 2},
        after=(upper, lower),
        us=2.4,
    )
    held = [left, upper, upper_in, lower, lower_in, anchor_v, moment_v]
    inner, new_first, new_second, new_anchor, new_momentum = call(
        functools.partial(outer_body, at),
        s,
        [Held(x) for x in held] + [*state, new_anchor, new_momentum],
        [hbm(rows, columns)] * 5,
        [vmem(2, rows, HEAD), dma((15,))],
        {len(held) + k: k for k in range(5)},
        us=2.0,
    )
    return (
        input_grad[None],
        inner[None],
        new_first[None],
        new_second[None],
        new_anchor,
        new_momentum,
    )


def solution(mesh):
    in_specs = (
        P("group", "fsdp", None),
        P("group", "fsdp", None),
        P("group", "fsdp", None),
        P("group", "fsdp", None),
        P("group", "fsdp", None),
        P("fsdp", None),
        P("fsdp", None),
        P(),
    )
    out_specs = (
        P("group", "fsdp", None),
        P("group", "fsdp", None),
        P("group", "fsdp", None),
        P("group", "fsdp", None),
        P("fsdp", None),
        P("fsdp", None),
    )
    short = mesh.shape["fsdp"] == 8 and mesh.shape["group"] == 4
    return jax.shard_map(
        line if short else plain,
        mesh=mesh,
        in_specs=in_specs,
        out_specs=out_specs,
        check_vma=False,
    )
```

```python
import functools

import jax
import jax.numpy as jnp
from jax import lax
from jax.experimental import pallas as pl
from jax.experimental.pallas import tpu as pltpu
from jax.sharding import PartitionSpec as P

HEAD = 128
STEP = 100
CORR_ONE = 1.0 - 0.9**STEP
CORR_TWO = 1.0 - 0.95**STEP
PARTS = ((0, 256), (256, 256))
TILE = 256
BF16 = jnp.bfloat16
F32 = jnp.float32


def plain(
    activations,
    cotangent,
    inner_weights,
    first_moment,
    second_moment,
    anchor,
    outer_momentum,
    fragment,
):
    tokens_in = activations[0]
    upstream = cotangent[0]
    weights = inner_weights[0]
    low_weights = weights.astype(BF16)
    input_grad = lax.dot_general(
        upstream,
        lax.all_gather(low_weights, "fsdp", axis=0, tiled=True),
        (((1,), (1,)), ((), ())),
        preferred_element_type=F32,
    ).astype(BF16)
    gradient = lax.psum_scatter(
        lax.dot_general(tokens_in, upstream, (((0,), (0,)), ((), ())), preferred_element_type=F32),
        "fsdp",
        scatter_dimension=0,
        tiled=True,
    )
    new_first = 0.9 * first_moment[0] + 0.1 * gradient
    new_second = 0.95 * second_moment[0] + 0.05 * gradient * gradient
    update = new_first / CORR_ONE / (jnp.sqrt(new_second / CORR_TWO) + 1e-08) + 0.1 * weights
    stepped = weights - 0.1 * update
    offset = fragment[0] * HEAD
    local_cols = lax.dynamic_slice_in_dim(stepped, offset, HEAD, 1)
    anchor_cols = lax.dynamic_slice_in_dim(anchor, offset, HEAD, 1)
    moment_cols = lax.dynamic_slice_in_dim(outer_momentum, offset, HEAD, 1)
    summed = lax.psum((anchor_cols - local_cols).astype(BF16), "group").astype(F32)
    average = summed / lax.axis_size("group")
    moment_new = 0.9 * moment_cols + average
    anchor_next = anchor_cols - 0.7 * (average + 0.9 * moment_new)
    new_momentum = lax.dynamic_update_slice_in_dim(outer_momentum, moment_new, offset, 1)
    new_anchor = lax.dynamic_update_slice_in_dim(anchor, anchor_next, offset, 1)
    new_inner = lax.dynamic_update_slice_in_dim(stepped, anchor_next, offset, 1)
    return (
        input_grad[None],
        new_inner[None],
        new_first[None],
        new_second[None],
        new_anchor,
        new_momentum,
    )


def rows_by_columns(act, cot):
    return lax.dot_general(act, cot, (((0,), (0,)), ((), ())), preferred_element_type=F32)


def vmem(*shape, dtype=F32):
    return pltpu.VMEM(shape, dtype)


def hbm(*shape, dtype=F32):
    return jax.ShapeDtypeStruct(shape, dtype)


class Numbers:
    def __init__(self, ref):
        self.ref, self.read = ref, {}

    def __getitem__(self, k):
        if k not in self.read:
            self.read[k] = self.ref[0, k]
        return self.read[k]


class Held:
    def __init__(self, array):
        self.array = array


def call(body, scalars, ins, outs, scratch=(), aliases=None, after=(), us=1.0):
    arrays, specs = [], []
    for x in [Held(scalars), *ins]:
        if isinstance(x, Held):
            arrays.append(pltpu.with_memory_space_constraint(x.array, pltpu.VMEM))
            specs.append(pl.BlockSpec(memory_space=pltpu.VMEM))
        else:
            arrays.append(pltpu.with_memory_space_constraint(x, pltpu.HBM))
            specs.append(pl.BlockSpec(memory_space=pltpu.HBM))
    first = len(arrays)
    arrays += [pltpu.with_memory_space_constraint(x, pltpu.VMEM) for x in after]
    specs += [pl.BlockSpec(memory_space=pltpu.VMEM)] * len(after)

    def inner(*refs):
        body(Numbers(refs[0]), *refs[1:first], *refs[first + len(after) :])

    return pl.pallas_call(
        inner,
        in_specs=specs,
        out_specs=[
            pl.BlockSpec(memory_space=pl.ANY if isinstance(o, jax.ShapeDtypeStruct) else pltpu.VMEM)
            for o in outs
        ],
        out_shape=list(outs),
        scratch_shapes=list(scratch),
        input_output_aliases={1 + k: v for k, v in (aliases or {}).items()},
        cost_estimate=pl.CostEstimate(
            flops=0, bytes_accessed=int(us * 3.4e6), transcendentals=0
        ),
        compiler_params=pltpu.CompilerParams(vmem_limit_bytes=12 * 1024 * 1024),
    )(*arrays)


def columns_of(ref, block, width):
    return ref.at[:, pl.ds(pl.multiple_of(block * width, width), width)]


def start(src, dst, sem):
    copy = pltpu.make_async_copy(src, dst, sem)
    copy.start()
    return copy


def pieces(head):
    return (0, HEAD, head), (HEAD, HEAD, head ^ 1), (2 * HEAD, 2 * HEAD, 1 - head // 2)


def turned(at, s, src, dst, sems, base, first=0):
    return [
        start(
            columns_of(src, s[at["pieces"] + k], width),
            dst.at[:, pl.ds(column + first, width)],
            sems.at[base + k],
        )
        for k, (column, width, _) in enumerate(pieces(0))
    ]


def cast_body(offset, s, w, low, wide, sems):
    rows, part = low.shape
    step = rows // 2
    copies = [
        start(
            w.at[pl.ds(i * step, step), pl.ds(offset, part)],
            wide.at[pl.ds(i * step, step)],
            sems.at[i],
        )
        for i in range(2)
    ]
    for i, copy in enumerate(copies):
        copy.wait()

        @pl.loop(0, step // 64)
        def _(n):
            here = pl.ds(pl.multiple_of(i * step + n * 64, 64), 64)
            low[here, :] = wide[here, :].astype(BF16)


def load_blocks(at, s, act, cot, act_s, cot_v, sems):
    heads = turned(at, s, cot, cot_v, sems, 0)
    rows = act_s.shape[2]
    blocks = [
        start(columns_of(act, 2 * d + s[at["core"]], rows), act_s.at[d], sems.at[len(heads) + d])
        for d in range(act_s.shape[0])
    ]
    return heads, blocks


def own_body(at, s, act, cot, anchor, moment, *rest):
    sums_ref, anchor_out, moment_out, act_s, cot_v, held, sems = rest
    chips, _, rows = act_s.shape
    heads, blocks = load_blocks(at, s, act, cot, act_s, cot_v, sems)
    base = len(heads) + chips
    loads = [start(src, held.at[k], sems.at[base + k]) for k, src in enumerate((anchor, moment))]
    stores = []
    for k, dst in enumerate((anchor_out, moment_out)):
        loads[k].wait()
        stores.append(start(held.at[k], dst, sems.at[base + 2 + k]))
    for copy in heads + blocks:
        copy.wait()

    @pl.loop(0, chips)
    def _(d):
        for i in range(rows // TILE):
            here = pl.ds(pl.multiple_of(d * rows + i * TILE, TILE), TILE)
            sums_ref[here, :] = rows_by_columns(
                act_s[d, :, i * TILE : (i + 1) * TILE], cot_v[...]
            )

    for copy in stores:
        copy.wait()


def sibling_body(at, s, before, act, cot, w, m, v, anchor, moment, *rest):
    sums_ref, w_v, m_v, v_v, anchor_v, moment_v, act_s, cot_v, sems = rest
    chips, _, rows = act_s.shape
    heads, blocks = load_blocks(at, s, act, cot, act_s, cot_v, sems)
    base = len(heads) + chips
    copies = []
    for src, dst in ((w, w_v), (m, m_v), (v, v_v)):
        copies += turned(at, s, src, dst, sems, base + len(copies))
    for src, dst in ((anchor, anchor_v), (moment, moment_v)):
        copies.append(
            start(columns_of(src, s[at["pieces"]], HEAD), dst, sems.at[base + len(copies)])
        )
    for copy in heads + blocks:
        copy.wait()

    @pl.loop(0, chips)
    def _(d):
        for i in range(rows // TILE):
            here = pl.ds(pl.multiple_of(d * rows + i * TILE, TILE), TILE)
            sums_ref[here, :] = before[here, :] + rows_by_columns(
                act_s[d, :, i * TILE : (i + 1) * TILE], cot_v[...]
            )

    for copy in copies:
        copy.wait()


def hop_body(at, step, offset, s, sums_ref, from_o, from_e, *rest):
    to_e, to_o, picked = rest[-3:]
    older = rest[0] if step == 3 else None
    rows, part = to_e.shape
    columns = slice(offset, offset + part)
    base = at["hop"] + 4 * (step - 1)
    size = 64

    def each(body):
        @pl.loop(0, rows // size)
        def _(i):
            body(pl.multiple_of(i * size, size))

    for mode, block, src, dst in (
        (s[base], s[base + 1], from_o, to_e),
        (s[base + 2], s[base + 3], from_e, to_o),
    ):
        first = pl.multiple_of(block * rows, rows)

        @pl.when(mode == 0)
        def _():
            def body(r):
                dst[pl.ds(r, size), :] = sums_ref[pl.ds(first + r, size), columns].astype(BF16)

            each(body)

        @pl.when(mode == 1)
        def _():
            def body(r):
                here = pl.ds(r, size)
                added = src[here, :].astype(F32) + sums_ref[pl.ds(first + r, size), columns]
                dst[here, :] = added.astype(BF16)

            each(body)

        @pl.when(mode == 2)
        def _():
            def body(r):
                dst[pl.ds(r, size), :] = src[pl.ds(r, size), :]

            each(body)

    def keep(src):
        def body(r):
            picked[pl.ds(r, size), :] = src[pl.ds(r, size), :]

        each(body)

    if step == 1:
        keep(from_e)
    else:

        @pl.when(s[at["middle"]] == 1)
        def _():
            keep(from_o if older is None else older)

        @pl.when(s[at["middle"]] == 0)
        def _():
            keep(from_e)


def grad_body(at, which, s, cot_own, cot_sib, *rest):
    theirs, out, token, stage, sems = rest[-5:]
    rows = stage.shape[1]
    copies = []
    if which > 0:
        copies.append(
            start(
                rest[len(PARTS)], columns_of(out, s[at["grad"] + 2 * which - 1], rows), sems.at[1]
            )
        )
    for cot, dst in ((cot_sib, theirs), (cot_own, stage)):
        for i in range(rows // TILE):
            here = slice(i * TILE, (i + 1) * TILE)
            total = None
            for (offset, part), block in zip(PARTS, rest):
                term = lax.dot_general(
                    cot[:, offset : offset + part],
                    block[here, :],
                    (((1,), (1,)), ((), ())),
                    preferred_element_type=F32,
                )
                total = term if total is None else total + term
            dst[:, here] = total.astype(BF16)
    copies.append(start(stage, columns_of(out, s[at["grad"] + 2 * which], rows), sems.at[0]))
    token[...] = jnp.zeros_like(token)
    for copy in copies:
        copy.wait()


def adam(at, offset, first_row, s, sums_ref, from_e, from_o, w, m, v, put, count, width, taken):
    columns = slice(offset, offset + width)
    size = 256
    base = pl.multiple_of(s[at["z"]] * from_e.shape[0], TILE)
    middle = s[at["middle"]] == 1

    @pl.loop(0, count // size)
    def _(i):
        r = pl.multiple_of(first_row + i * size, size)
        here = pl.ds(r, size)
        one = sums_ref[pl.ds(base + r, size), columns] + from_e[here, taken].astype(F32)
        both = one + from_o[here, taken].astype(F32)
        gradient = jnp.where(middle, both, one)
        first = 0.9 * m[here, columns] + 0.1 * gradient
        second = 0.95 * v[here, columns] + 0.05 * gradient * gradient
        below = second * lax.rsqrt(second) + 1e-08 * CORR_TWO**0.5
        moved = first * (0.1 * CORR_TWO**0.5 / CORR_ONE) / below
        stepped = (1.0 - 0.1 * 0.1) * w[here, columns] - moved
        put(r, stepped, first, second)


def head_body(at, s, sums_ref, from_e, from_o, w, m, v, anchor, upper, lower, first_v, second_v):
    rows = anchor.shape[0]
    for k, diff in enumerate((upper, lower)):
        top = k * rows // 2

        def put(r, stepped, first, second):
            here = pl.ds(r, stepped.shape[0])
            first_v[here, :] = first
            second_v[here, :] = second
            there = pl.ds(r - top, stepped.shape[0])
            diff[there, :] = (anchor[here, :] - stepped).astype(BF16)

        args = (from_e, from_o, w, m, v, put, rows // 2, HEAD, slice(0, HEAD))
        adam(at, 0, top, s, sums_ref, *args)


def rest_body(at, offset, part, within, s, sums_ref, from_e, from_o, w, m, v, *rest):
    stage, sems = rest[-2:]
    rows = from_e.shape[0]
    tiles = rows // TILE
    copies = []
    if within:
        first_v, second_v, theirs = rest[:3]
        *outs, grads, token = rest[4:-2]
        for k, src in enumerate((first_v, second_v)):
            there = columns_of(outs[1 + k], s[at["pieces"]], HEAD)
            copies.append(start(src, there, sems.at[k]))
        copies.append(start(theirs, columns_of(grads, s[at["grad"] + 7], rows), sems.at[2]))
        token[...] = jnp.zeros_like(token)
    else:
        tiles -= 1
        *outs, left = rest[3:-2]
    piece = next(k for k, (column, *_) in enumerate(pieces(0)) if column == offset)
    args = (from_e, from_o, w, m, v)
    taken = slice(within, within + part)

    def putter(refs, top):
        def put(r, *values):
            here = pl.ds(r - top, values[0].shape[0])
            for k, value in enumerate(values):
                refs[k, here, :] = value

        return put

    for tile in range(tiles):
        first = tile * TILE
        adam(at, offset, first, s, sums_ref, *args, putter(stage, 0), TILE, part, taken)
        there = pl.ds(first, TILE)
        for k, out in enumerate(outs):
            copies.append(
                start(
                    stage.at[k, there],
                    columns_of(out.at[there], s[at["pieces"] + piece], part),
                    sems.at[len(copies)],
                )
            )
    if not within:
        first = tiles * TILE
        adam(at, offset, first, s, sums_ref, *args, putter(left, first), TILE, part, taken)
    for copy in copies:
        copy.wait()


def mix_body(s, own, other, out):
    size = 128

    @pl.loop(0, out.shape[0] // size)
    def _(i):
        here = pl.ds(pl.multiple_of(i * size, size), size)
        out[here, :] = (own[here, :].astype(F32) + other[here, :].astype(F32)).astype(BF16)


def outer_body(at, s, left, upper, upper_in, lower, lower_in, anchor, moment, *rest):
    inner, first, second, new_anchor, new_moment, stage, sems = rest[5:]
    rows = anchor.shape[0]
    _, count, part = left.shape
    there = pl.ds(rows - count, count)
    copies = []
    for k, out in enumerate((inner, first, second)):
        last = columns_of(out.at[there], s[at["pieces"] + 2], part)
        copies.append(start(left.at[k], last, sems.at[k]))
    half = rows // 2
    size = half // 2
    for n, (own, other) in enumerate(((upper, upper_in), (lower, lower_in))):
        for r in (0, size):
            here, there = pl.ds(r, size), pl.ds(n * half + r, size)
            average = (own[here, :].astype(F32) + other[here, :].astype(F32)) * 0.25
            momentum = 0.9 * moment[there, :] + average
            stage[0, there, :] = momentum
            stage[1, there, :] = anchor[there, :] - 0.7 * (average + 0.9 * momentum)
            for k, out in ((0, new_moment), (1, new_anchor), (1, inner)):
                target = columns_of(out.at[there], s[at["pieces"]], HEAD)
                copies.append(start(stage.at[k, there], target, sems.at[len(copies)]))
    for copy in copies:
        copy.wait()


def line(
    activations,
    cotangent,
    inner_weights,
    first_moment,
    second_moment,
    anchor,
    outer_momentum,
    fragment,
):
    act, cot, weights = activations[0], cotangent[0], inner_weights[0]
    moment, second = first_moment[0], second_moment[0]
    tokens, width = act.shape
    rows, columns = weights.shape
    chips = lax.axis_size("fsdp") // 2
    me = lax.axis_index("fsdp")
    z, core = me // 2, me % 2
    head = fragment[0]
    last = chips - 1
    middle = (z > 0) & (z < last)
    even = z % 2 == 0
    zd = last - z

    def cross(i):
        return i ^ 1 if i // 2 in (0, last) else (i + 2 if i // 2 % 2 else i - 2)

    e_perm = [(i, i ^ 2) for i in range(2 * chips)]
    o_perm = [(i, cross(i)) for i in range(2 * chips)]
    swap = [(i, i ^ 1) for i in range(2 * chips)]
    x_perm, y_perm = [(i, i ^ 1) for i in range(4)], [(i, i ^ 2) for i in range(4)]

    values, at = [], {}

    def name(key, *numbers):
        at[key] = len(values)
        values.extend(jnp.asarray(v, jnp.int32) for v in numbers)

    name("z", z)
    name("core", core)
    name("middle", middle)
    name("pieces", *[block for _, _, block in pieces(head)])
    name("grad", *[2 * (z ^ k) + c for k in range(chips) for c in (core, 1 - core)])
    hops = []
    for step in range(1, chips):
        up_mode = jnp.where(step <= z, 2, jnp.where(z == 0, 0, 1))
        down_mode = jnp.where(step <= zd, 2, jnp.where(zd == 0, 0, 1))
        up_to = jnp.clip(chips - step + z, 0, last)
        down_to = jnp.clip(step - 1 - zd, 0, last)
        hops += [
            jnp.where(even, up_mode, down_mode),
            jnp.where(even, up_to, down_to),
            jnp.where(middle, jnp.where(even, down_mode, up_mode), 2),
            jnp.where(even, down_to, up_to),
        ]
    name("hop", *hops)
    s = jnp.pad(jnp.stack(values), (0, 128 - len(values)))[None]

    def permute(x, perm, axis="fsdp"):
        return lax.ppermute(x, axis, perm)

    dma = pltpu.SemaphoreType.DMA
    from_e, from_o = [[]], [[]]
    act_sib, cot_sib = permute(act, swap), permute(cot, swap)
    (_, first), (offset, part) = PARTS
    low = [weights[:, :first].astype(BF16)]
    low += call(
        functools.partial(cast_body, offset),
        s,
        [weights],
        [vmem(rows, part, dtype=BF16)],
        [vmem(rows, part), dma((2,))],
        after=[cot_sib],
        us=2.0,
    )
    for x in low:
        from_e[0].append(permute(x, e_perm))
        from_o[0].append(permute(x, o_perm))

    sums_shape = vmem(chips * rows, columns)
    cot_shape = vmem(tokens, columns, dtype=BF16)
    block_shape = vmem(chips, tokens, rows, dtype=BF16)
    sums_own, new_anchor, new_momentum = call(
        functools.partial(own_body, at),
        s,
        [act, Held(cot), anchor, outer_momentum],
        [sums_shape, hbm(rows, columns), hbm(rows, columns)],
        [block_shape, cot_shape, vmem(2, rows, columns), dma((chips + 7,))],
        after=low[-1:],
        us=5.0,
    )
    sums_both, w_v, m_v, v_v, anchor_v, moment_v = call(
        functools.partial(sibling_body, at),
        s,
        [Held(sums_own), act_sib, Held(cot_sib), weights, moment, second, anchor, outer_momentum],
        [sums_shape] + [vmem(rows, columns)] * 3 + [vmem(rows, HEAD)] * 2,
        [block_shape, cot_shape, dma((chips + 14,))],
        {0: 0},
        us=5.0,
    )

    def hop(step, j, after):
        offset, part = PARTS[j]
        ins = [Held(sums_both), Held(from_o[step - 1][j]), Held(from_e[step - 1][j])]
        if step == 3:
            ins += [Held(from_o[0][j])]
        return call(
            functools.partial(hop_body, at, step, offset),
            s,
            ins,
            [vmem(rows, part, dtype=BF16)] * 3,
            after=after,
        )

    def grad(which, before, own, after):
        ins = [Held(x) for x in [cot, cot_sib, *own]]
        aliases = {}
        if before is not None:
            theirs, buffer = before
            ins += [Held(theirs)]
            aliases = {len(ins): 1}
            ins += [buffer]
        theirs, buffer, token = call(
            functools.partial(grad_body, at, which),
            s,
            ins,
            [
                vmem(tokens, rows, dtype=BF16),
                hbm(tokens, width, dtype=BF16),
                vmem(8, 128),
            ],
            [vmem(tokens, rows, dtype=BF16), dma((2,))],
            aliases,
            after,
            us=2.1,
        )
        return (permute(theirs, swap), buffer), token

    grads, after, picked = None, (), low
    for step in range(1, chips):
        from_e.append([])
        from_o.append([])
        found = []
        for j in range(len(PARTS)):
            to_e, to_o, pick = hop(step, j, after)
            from_e[step].append(permute(to_e, e_perm))
            from_o[step].append(permute(to_o, o_perm))
            found.append(pick)
            after = ()
            if j == 0:
                grads, token = grad(step - 1, grads, picked, (to_e,))
                after = (token,)
        picked = found
    grads, token = grad(last, grads, picked, ())

    theirs, input_grad = grads
    half = vmem(rows // 2, HEAD, dtype=BF16)
    full = [hbm(rows, columns)] * 3

    def inputs(j):
        return [sums_both, from_e[last][j], from_o[last][j], w_v, m_v, v_v]

    upper, lower, first_v, second_v = call(
        functools.partial(head_body, at),
        s,
        [Held(x) for x in [*inputs(0), anchor_v]],
        [half, half, vmem(rows, HEAD), vmem(rows, HEAD)],
        after=(token,),
        us=1.0,
    )
    upper_in = permute(upper, x_perm, "group")
    lower_in = permute(lower, y_perm, "group")
    *state, input_grad, token = call(
        functools.partial(rest_body, at, HEAD, PARTS[0][1] - HEAD, HEAD),
        s,
        [Held(x) for x in [*inputs(0), first_v, second_v, theirs]] + [input_grad],
        full + [hbm(tokens, width, dtype=BF16), vmem(8, 128)],
        [vmem(3, rows, PARTS[0][1] - HEAD), dma((3 + 3 * rows // TILE,))],
        {9: 3},
        us=2.0,
    )
    upper = call(mix_body, s, [Held(upper), Held(upper_in)], [half], after=(token,), us=0.5)[0]
    upper_in = permute(upper, y_perm, "group")
    lower = call(mix_body, s, [Held(lower), Held(lower_in)], [half], after=(upper,), us=0.5)[0]
    lower_in = permute(lower, x_perm, "group")
    offset, part = PARTS[1]
    *state, left = call(
        functools.partial(rest_body, at, offset, part, 0),
        s,
        [Held(x) for x in inputs(1)] + state,
        full + [vmem(3, TILE, part)],
        [vmem(3, rows, part), dma((3 * rows // TILE,))],
        {6: 0, 7: 1, 8: 2},
        after=(upper, lower),
        us=2.4,
    )
    held = [left, upper, upper_in, lower, lower_in, anchor_v, moment_v]
    inner, new_first, new_second, new_anchor, new_momentum = call(
        functools.partial(outer_body, at),
        s,
        [Held(x) for x in held] + [*state, new_anchor, new_momentum],
        [hbm(rows, columns)] * 5,
        [vmem(2, rows, HEAD), dma((15,))],
        {len(held) + k: k for k in range(5)},
        us=2.0,
    )
    return (
        input_grad[None],
        inner[None],
        new_first[None],
        new_second[None],
        new_anchor,
        new_momentum,
    )


def solution(mesh):
    in_specs = (
        P("group", "fsdp", None),
        P("group", "fsdp", None),
        P("group", "fsdp", None),
        P("group", "fsdp", None),
        P("group", "fsdp", None),
        P("fsdp", None),
        P("fsdp", None),
        P(),
    )
    out_specs = (
        P("group", "fsdp", None),
        P("group", "fsdp", None),
        P("group", "fsdp", None),
        P("group", "fsdp", None),
        P("fsdp", None),
        P("fsdp", None),
    )
    short = mesh.shape["fsdp"] == 8 and mesh.shape["group"] == 4
    return jax.shard_map(
        line if short else plain,
        mesh=mesh,
        in_specs=in_specs,
        out_specs=out_specs,
        check_vma=False,
    )
```

```python
import functools

import jax
import jax.numpy as jnp
from jax import lax
from jax.experimental import pallas as pl
from jax.experimental.pallas import tpu as pltpu
from jax.sharding import PartitionSpec as P

HEAD = 128
STEP = 100
CORR_ONE = 1.0 - 0.9**STEP
CORR_TWO = 1.0 - 0.95**STEP
PARTS = ((0, 256), (256, 256))
TILE = 256
BF16 = jnp.bfloat16
F32 = jnp.float32


def plain(
    activations,
    cotangent,
    inner_weights,
    first_moment,
    second_moment,
    anchor,
    outer_momentum,
    fragment,
):
    tokens_in = activations[0]
    upstream = cotangent[0]
    weights = inner_weights[0]
    low_weights = weights.astype(BF16)
    input_grad = lax.dot_general(
        upstream,
        lax.all_gather(low_weights, "fsdp", axis=0, tiled=True),
        (((1,), (1,)), ((), ())),
        preferred_element_type=F32,
    ).astype(BF16)
    gradient = lax.psum_scatter(
        lax.dot_general(tokens_in, upstream, (((0,), (0,)), ((), ())), preferred_element_type=F32),
        "fsdp",
        scatter_dimension=0,
        tiled=True,
    )
    new_first = 0.9 * first_moment[0] + 0.1 * gradient
    new_second = 0.95 * second_moment[0] + 0.05 * gradient * gradient
    update = new_first / CORR_ONE / (jnp.sqrt(new_second / CORR_TWO) + 1e-08) + 0.1 * weights
    stepped = weights - 0.1 * update
    offset = fragment[0] * HEAD
    local_cols = lax.dynamic_slice_in_dim(stepped, offset, HEAD, 1)
    anchor_cols = lax.dynamic_slice_in_dim(anchor, offset, HEAD, 1)
    moment_cols = lax.dynamic_slice_in_dim(outer_momentum, offset, HEAD, 1)
    summed = lax.psum((anchor_cols - local_cols).astype(BF16), "group").astype(F32)
    average = summed / lax.axis_size("group")
    moment_new = 0.9 * moment_cols + average
    anchor_next = anchor_cols - 0.7 * (average + 0.9 * moment_new)
    new_momentum = lax.dynamic_update_slice_in_dim(outer_momentum, moment_new, offset, 1)
    new_anchor = lax.dynamic_update_slice_in_dim(anchor, anchor_next, offset, 1)
    new_inner = lax.dynamic_update_slice_in_dim(stepped, anchor_next, offset, 1)
    return (
        input_grad[None],
        new_inner[None],
        new_first[None],
        new_second[None],
        new_anchor,
        new_momentum,
    )


def rows_by_columns(act, cot):
    return lax.dot_general(act, cot, (((0,), (0,)), ((), ())), preferred_element_type=F32)


def vmem(*shape, dtype=F32):
    return pltpu.VMEM(shape, dtype)


def hbm(*shape, dtype=F32):
    return jax.ShapeDtypeStruct(shape, dtype)


class Numbers:
    def __init__(self, ref):
        self.ref, self.read = ref, {}

    def __getitem__(self, k):
        if k not in self.read:
            self.read[k] = self.ref[0, k]
        return self.read[k]


class Held:
    def __init__(self, array):
        self.array = array


def call(body, scalars, ins, outs, scratch=(), aliases=None, after=(), us=1.0):
    arrays, specs = [], []
    for x in [*([] if scalars is None else [Held(scalars)]), *ins]:
        if isinstance(x, Held):
            arrays.append(pltpu.with_memory_space_constraint(x.array, pltpu.VMEM))
            specs.append(pl.BlockSpec(memory_space=pltpu.VMEM))
        else:
            arrays.append(pltpu.with_memory_space_constraint(x, pltpu.HBM))
            specs.append(pl.BlockSpec(memory_space=pltpu.HBM))
    first = len(arrays)
    arrays += [pltpu.with_memory_space_constraint(x, pltpu.VMEM) for x in after]
    specs += [pl.BlockSpec(memory_space=pltpu.VMEM)] * len(after)

    def inner(*refs):
        rest = refs[:first] + refs[first + len(after) :]
        body(*rest) if scalars is None else body(Numbers(rest[0]), *rest[1:])

    return pl.pallas_call(
        inner,
        in_specs=specs,
        out_specs=[
            pl.BlockSpec(memory_space=pl.ANY if isinstance(o, jax.ShapeDtypeStruct) else pltpu.VMEM)
            for o in outs
        ],
        out_shape=list(outs),
        scratch_shapes=list(scratch),
        input_output_aliases={1 + k: v for k, v in (aliases or {}).items()},
        cost_estimate=pl.CostEstimate(
            flops=0, bytes_accessed=int(us * 3.4e6), transcendentals=0
        ),
        compiler_params=pltpu.CompilerParams(vmem_limit_bytes=12 * 1024 * 1024),
    )(*arrays)


def columns_of(ref, block, width):
    return ref.at[:, pl.ds(pl.multiple_of(block * width, width), width)]


def start(src, dst, sem):
    copy = pltpu.make_async_copy(src, dst, sem)
    copy.start()
    return copy


def pieces(head):
    return (0, HEAD, head), (HEAD, HEAD, head ^ 1), (2 * HEAD, 2 * HEAD, 1 - head // 2)


def turned(at, s, src, dst, sems, base, first=0):
    return [
        start(
            columns_of(src, s[at["pieces"] + k], width),
            dst.at[:, pl.ds(column + first, width)],
            sems.at[base + k],
        )
        for k, (column, width, _) in enumerate(pieces(0))
    ]


def cast_body(offset, w, low, wide, sems):
    rows, part = low.shape
    chunks = 4
    step = rows // chunks
    copies = [
        start(
            w.at[pl.ds(i * step, step), pl.ds(offset, part)],
            wide.at[pl.ds(i * step, step)],
            sems.at[i],
        )
        for i in range(chunks)
    ]
    for i, copy in enumerate(copies):
        copy.wait()

        @pl.loop(0, step // 64)
        def _(n):
            here = pl.ds(pl.multiple_of(i * step + n * 64, 64), 64)
            low[here, :] = wide[here, :].astype(BF16)


def load_blocks(at, s, act, cot, act_s, cot_v, sems):
    heads = turned(at, s, cot, cot_v, sems, 0)
    rows = act_s.shape[2]
    blocks = [
        start(columns_of(act, 2 * d + s[at["core"]], rows), act_s.at[d], sems.at[len(heads) + d])
        for d in range(act_s.shape[0])
    ]
    return heads, blocks


def own_body(at, s, act, cot, anchor, moment, *rest):
    sums_ref, anchor_out, moment_out, act_s, cot_v, held, sems = rest
    chips, _, rows = act_s.shape
    heads, blocks = load_blocks(at, s, act, cot, act_s, cot_v, sems)
    base = len(heads) + chips
    loads = [start(src, held.at[k], sems.at[base + k]) for k, src in enumerate((anchor, moment))]
    stores = []
    for k, dst in enumerate((anchor_out, moment_out)):
        loads[k].wait()
        stores.append(start(held.at[k], dst, sems.at[base + 2 + k]))
    for copy in heads + blocks:
        copy.wait()

    @pl.loop(0, chips)
    def _(d):
        for i in range(rows // TILE):
            here = pl.ds(pl.multiple_of(d * rows + i * TILE, TILE), TILE)
            sums_ref[here, :] = rows_by_columns(
                act_s[d, :, i * TILE : (i + 1) * TILE], cot_v[...]
            )

    for copy in stores:
        copy.wait()


def sibling_body(at, s, before, act, cot, w, m, v, anchor, moment, *rest):
    sums_ref, w_v, m_v, v_v, anchor_v, moment_v, act_s, cot_v, sems = rest
    chips, _, rows = act_s.shape
    heads, blocks = load_blocks(at, s, act, cot, act_s, cot_v, sems)
    base = len(heads) + chips
    copies = []
    for src, dst in ((w, w_v), (m, m_v), (v, v_v)):
        copies += turned(at, s, src, dst, sems, base + len(copies))
    for src, dst in ((anchor, anchor_v), (moment, moment_v)):
        copies.append(
            start(columns_of(src, s[at["pieces"]], HEAD), dst, sems.at[base + len(copies)])
        )
    for copy in heads + blocks:
        copy.wait()

    @pl.loop(0, chips)
    def _(d):
        for i in range(rows // TILE):
            here = pl.ds(pl.multiple_of(d * rows + i * TILE, TILE), TILE)
            sums_ref[here, :] = before[here, :] + rows_by_columns(
                act_s[d, :, i * TILE : (i + 1) * TILE], cot_v[...]
            )

    for copy in copies:
        copy.wait()


def hop_body(at, step, offset, s, sums_ref, from_o, from_e, *rest):
    to_e, to_o, picked = rest[-3:]
    older = rest[0] if step == 3 else None
    rows, part = to_e.shape
    columns = slice(offset, offset + part)
    base = at["hop"] + 4 * (step - 1)
    size = 64

    def each(body):
        @pl.loop(0, rows // size)
        def _(i):
            body(pl.multiple_of(i * size, size))

    for mode, block, src, dst in (
        (s[base], s[base + 1], from_o, to_e),
        (s[base + 2], s[base + 3], from_e, to_o),
    ):
        first = pl.multiple_of(block * rows, rows)

        @pl.when(mode == 0)
        def _():
            def body(r):
                dst[pl.ds(r, size), :] = sums_ref[pl.ds(first + r, size), columns].astype(BF16)

            each(body)

        @pl.when(mode == 1)
        def _():
            def body(r):
                here = pl.ds(r, size)
                added = src[here, :].astype(F32) + sums_ref[pl.ds(first + r, size), columns]
                dst[here, :] = added.astype(BF16)

            each(body)

        @pl.when(mode == 2)
        def _():
            def body(r):
                dst[pl.ds(r, size), :] = src[pl.ds(r, size), :]

            each(body)

    def keep(src):
        def body(r):
            picked[pl.ds(r, size), :] = src[pl.ds(r, size), :]

        each(body)

    if step == 1:
        keep(from_e)
    else:

        @pl.when(s[at["middle"]] == 1)
        def _():
            keep(from_o if older is None else older)

        @pl.when(s[at["middle"]] == 0)
        def _():
            keep(from_e)


def grad_body(at, which, s, cot_own, cot_sib, *rest):
    theirs, out, token, stage, sems = rest[-5:]
    rows = stage.shape[1]
    copies = []
    if which > 0:
        copies.append(
            start(
                rest[len(PARTS)], columns_of(out, s[at["grad"] + 2 * which - 1], rows), sems.at[1]
            )
        )
    for cot, dst in ((cot_sib, theirs), (cot_own, stage)):
        for i in range(rows // TILE):
            here = slice(i * TILE, (i + 1) * TILE)
            total = None
            for (offset, part), block in zip(PARTS, rest):
                term = lax.dot_general(
                    cot[:, offset : offset + part],
                    block[here, :],
                    (((1,), (1,)), ((), ())),
                    preferred_element_type=F32,
                )
                total = term if total is None else total + term
            dst[:, here] = total.astype(BF16)
    copies.append(start(stage, columns_of(out, s[at["grad"] + 2 * which], rows), sems.at[0]))
    token[...] = jnp.zeros_like(token)
    for copy in copies:
        copy.wait()


def adam(at, offset, first_row, s, sums_ref, from_e, from_o, w, m, v, put, count, width, taken):
    columns = slice(offset, offset + width)
    size = 256
    base = pl.multiple_of(s[at["z"]] * from_e.shape[0], TILE)
    middle = s[at["middle"]] == 1

    @pl.loop(0, count // size)
    def _(i):
        r = pl.multiple_of(first_row + i * size, size)
        here = pl.ds(r, size)
        one = sums_ref[pl.ds(base + r, size), columns] + from_e[here, taken].astype(F32)
        both = one + from_o[here, taken].astype(F32)
        gradient = jnp.where(middle, both, one)
        first = 0.9 * m[here, columns] + 0.1 * gradient
        second = 0.95 * v[here, columns] + 0.05 * gradient * gradient
        below = second * lax.rsqrt(second) + 1e-08 * CORR_TWO**0.5
        moved = first * (0.1 * CORR_TWO**0.5 / CORR_ONE) / below
        stepped = (1.0 - 0.1 * 0.1) * w[here, columns] - moved
        put(r, stepped, first, second)


def head_body(at, s, sums_ref, from_e, from_o, w, m, v, anchor, upper, lower, first_v, second_v):
    rows = anchor.shape[0]
    for k, diff in enumerate((upper, lower)):
        top = k * rows // 2

        def put(r, stepped, first, second):
            here = pl.ds(r, stepped.shape[0])
            first_v[here, :] = first
            second_v[here, :] = second
            there = pl.ds(r - top, stepped.shape[0])
            diff[there, :] = (anchor[here, :] - stepped).astype(BF16)

        args = (from_e, from_o, w, m, v, put, rows // 2, HEAD, slice(0, HEAD))
        adam(at, 0, top, s, sums_ref, *args)


def rest_body(at, offset, part, within, s, sums_ref, from_e, from_o, w, m, v, *rest):
    stage, sems = rest[-2:]
    rows = from_e.shape[0]
    tiles = rows // TILE
    copies = []
    if within:
        first_v, second_v, theirs = rest[:3]
        *outs, grads, token = rest[4:-2]
        for k, src in enumerate((first_v, second_v)):
            there = columns_of(outs[1 + k], s[at["pieces"]], HEAD)
            copies.append(start(src, there, sems.at[k]))
        copies.append(start(theirs, columns_of(grads, s[at["grad"] + 7], rows), sems.at[2]))
        token[...] = jnp.zeros_like(token)
    else:
        tiles -= 1
        *outs, left = rest[3:-2]
    piece = next(k for k, (column, *_) in enumerate(pieces(0)) if column == offset)
    args = (from_e, from_o, w, m, v)
    taken = slice(within, within + part)

    def putter(refs, top):
        def put(r, *values):
            here = pl.ds(r - top, values[0].shape[0])
            for k, value in enumerate(values):
                refs[k, here, :] = value

        return put

    for tile in range(tiles):
        first = tile * TILE
        adam(at, offset, first, s, sums_ref, *args, putter(stage, 0), TILE, part, taken)
        there = pl.ds(first, TILE)
        for k, out in enumerate(outs):
            copies.append(
                start(
                    stage.at[k, there],
                    columns_of(out.at[there], s[at["pieces"] + piece], part),
                    sems.at[len(copies)],
                )
            )
    if not within:
        first = tiles * TILE
        adam(at, offset, first, s, sums_ref, *args, putter(left, first), TILE, part, taken)
    for copy in copies:
        copy.wait()


def mix(own, other, token):
    return (own.astype(F32) + other.astype(F32) + token[:1]).astype(BF16)


def outer_body(at, s, left, upper, upper_in, lower, lower_in, anchor, moment, *rest):
    inner, first, second, new_anchor, new_moment, stage, sems = rest[5:]
    rows = anchor.shape[0]
    _, count, part = left.shape
    there = pl.ds(rows - count, count)
    copies = []
    for k, out in enumerate((inner, first, second)):
        last = columns_of(out.at[there], s[at["pieces"] + 2], part)
        copies.append(start(left.at[k], last, sems.at[k]))
    half = rows // 2
    size = half // 2
    for n, (own, other) in enumerate(((upper, upper_in), (lower, lower_in))):
        for r in (0, size):
            here, there = pl.ds(r, size), pl.ds(n * half + r, size)
            average = (own[here, :].astype(F32) + other[here, :].astype(F32)) * 0.25
            momentum = 0.9 * moment[there, :] + average
            stage[0, there, :] = momentum
            stage[1, there, :] = anchor[there, :] - 0.7 * (average + 0.9 * momentum)
            for k, out in ((0, new_moment), (1, new_anchor), (1, inner)):
                target = columns_of(out.at[there], s[at["pieces"]], HEAD)
                copies.append(start(stage.at[k, there], target, sems.at[len(copies)]))
    for copy in copies:
        copy.wait()


def line(
    activations,
    cotangent,
    inner_weights,
    first_moment,
    second_moment,
    anchor,
    outer_momentum,
    fragment,
):
    act, cot, weights = activations[0], cotangent[0], inner_weights[0]
    moment, second = first_moment[0], second_moment[0]
    tokens, width = act.shape
    rows, columns = weights.shape
    chips = lax.axis_size("fsdp") // 2
    me = lax.axis_index("fsdp")
    z, core = me // 2, me % 2
    head = fragment[0]
    last = chips - 1
    middle = (z > 0) & (z < last)
    even = z % 2 == 0
    zd = last - z

    def cross(i):
        return i ^ 1 if i // 2 in (0, last) else (i + 2 if i // 2 % 2 else i - 2)

    e_perm = [(i, i ^ 2) for i in range(2 * chips)]
    o_perm = [(i, cross(i)) for i in range(2 * chips)]
    swap = [(i, i ^ 1) for i in range(2 * chips)]
    x_perm, y_perm = [(i, i ^ 1) for i in range(4)], [(i, i ^ 2) for i in range(4)]

    values, at = [], {}

    def name(key, *numbers):
        at[key] = len(values)
        values.extend(jnp.asarray(v, jnp.int32) for v in numbers)

    name("z", z)
    name("core", core)
    name("middle", middle)
    name("pieces", *[block for _, _, block in pieces(head)])
    name("grad", *[2 * (z ^ k) + c for k in range(chips) for c in (core, 1 - core)])
    hops = []
    for step in range(1, chips):
        up_mode = jnp.where(step <= z, 2, jnp.where(z == 0, 0, 1))
        down_mode = jnp.where(step <= zd, 2, jnp.where(zd == 0, 0, 1))
        up_to = jnp.clip(chips - step + z, 0, last)
        down_to = jnp.clip(step - 1 - zd, 0, last)
        hops += [
            jnp.where(even, up_mode, down_mode),
            jnp.where(even, up_to, down_to),
            jnp.where(middle, jnp.where(even, down_mode, up_mode), 2),
            jnp.where(even, down_to, up_to),
        ]
    name("hop", *hops)
    s = jnp.pad(jnp.stack(values), (0, 128 - len(values)))[None]

    def permute(x, perm, axis="fsdp"):
        return lax.ppermute(x, axis, perm)

    dma = pltpu.SemaphoreType.DMA
    from_e, from_o = [[]], [[]]
    act_sib, cot_sib = permute(act, swap), permute(cot, swap)
    low = []
    for (offset, part), after in zip(PARTS, ([], [cot_sib])):
        low += call(
            functools.partial(cast_body, offset),
            None,
            [weights],
            [vmem(rows, part, dtype=BF16)],
            [vmem(rows, part), dma((4,))],
            after=after,
            us=1.2,
        )
    for x in low:
        from_e[0].append(permute(x, e_perm))
        from_o[0].append(permute(x, o_perm))

    sums_shape = vmem(chips * rows, columns)
    cot_shape = vmem(tokens, columns, dtype=BF16)
    block_shape = vmem(chips, tokens, rows, dtype=BF16)
    sums_own, new_anchor, new_momentum = call(
        functools.partial(own_body, at),
        s,
        [act, Held(cot), anchor, outer_momentum],
        [sums_shape, hbm(rows, columns), hbm(rows, columns)],
        [block_shape, cot_shape, vmem(2, rows, columns), dma((chips + 7,))],
        after=low[-1:],
        us=5.0,
    )
    sums_both, w_v, m_v, v_v, anchor_v, moment_v = call(
        functools.partial(sibling_body, at),
        s,
        [Held(sums_own), act_sib, Held(cot_sib), weights, moment, second, anchor, outer_momentum],
        [sums_shape] + [vmem(rows, columns)] * 3 + [vmem(rows, HEAD)] * 2,
        [block_shape, cot_shape, dma((chips + 14,))],
        {0: 0},
        us=5.0,
    )

    def hop(step, j, after):
        offset, part = PARTS[j]
        ins = [Held(sums_both), Held(from_o[step - 1][j]), Held(from_e[step - 1][j])]
        if step == 3:
            ins += [Held(from_o[0][j])]
        return call(
            functools.partial(hop_body, at, step, offset),
            s,
            ins,
            [vmem(rows, part, dtype=BF16)] * 3,
            after=after,
        )

    def grad(which, before, own, after):
        ins = [Held(x) for x in [cot, cot_sib, *own]]
        aliases = {}
        if before is not None:
            theirs, buffer = before
            ins += [Held(theirs)]
            aliases = {len(ins): 1}
            ins += [buffer]
        theirs, buffer, token = call(
            functools.partial(grad_body, at, which),
            s,
            ins,
            [
                vmem(tokens, rows, dtype=BF16),
                hbm(tokens, width, dtype=BF16),
                vmem(8, 128),
            ],
            [vmem(tokens, rows, dtype=BF16), dma((2,))],
            aliases,
            after,
            us=2.1,
        )
        return (permute(theirs, swap), buffer), token

    grads, after, picked = None, (), low
    for step in range(1, chips):
        from_e.append([])
        from_o.append([])
        found = []
        for j in range(len(PARTS)):
            to_e, to_o, pick = hop(step, j, after)
            from_e[step].append(permute(to_e, e_perm))
            from_o[step].append(permute(to_o, o_perm))
            found.append(pick)
            after = ()
            if j == 0:
                grads, token = grad(step - 1, grads, picked, (to_e,))
                after = (token,)
        picked = found
    grads, token = grad(last, grads, picked, ())

    theirs, input_grad = grads
    half = vmem(rows // 2, HEAD, dtype=BF16)
    full = [hbm(rows, columns)] * 3

    def inputs(j):
        return [sums_both, from_e[last][j], from_o[last][j], w_v, m_v, v_v]

    upper, lower, first_v, second_v = call(
        functools.partial(head_body, at),
        s,
        [Held(x) for x in [*inputs(0), anchor_v]],
        [half, half, vmem(rows, HEAD), vmem(rows, HEAD)],
        after=(token,),
        us=1.0,
    )
    upper_in = permute(upper, x_perm, "group")
    lower_in = permute(lower, y_perm, "group")
    *state, input_grad, token = call(
        functools.partial(rest_body, at, HEAD, PARTS[0][1] - HEAD, HEAD),
        s,
        [Held(x) for x in [*inputs(0), first_v, second_v, theirs]] + [input_grad],
        full + [hbm(tokens, width, dtype=BF16), vmem(8, 128)],
        [vmem(3, rows, PARTS[0][1] - HEAD), dma((3 + 3 * rows // TILE,))],
        {9: 3},
        us=2.0,
    )
    upper, lower = mix(upper, upper_in, token), mix(lower, lower_in, token)
    upper_in = permute(upper, y_perm, "group")
    lower_in = permute(lower, x_perm, "group")
    offset, part = PARTS[1]
    *state, left = call(
        functools.partial(rest_body, at, offset, part, 0),
        s,
        [Held(x) for x in inputs(1)] + state,
        full + [vmem(3, TILE, part)],
        [vmem(3, rows, part), dma((3 * rows // TILE,))],
        {6: 0, 7: 1, 8: 2},
        after=(upper, lower),
        us=2.4,
    )
    held = [left, upper, upper_in, lower, lower_in, anchor_v, moment_v]
    inner, new_first, new_second, new_anchor, new_momentum = call(
        functools.partial(outer_body, at),
        s,
        [Held(x) for x in held] + [*state, new_anchor, new_momentum],
        [hbm(rows, columns)] * 5,
        [vmem(2, rows, HEAD), dma((15,))],
        {len(held) + k: k for k in range(5)},
        us=2.0,
    )
    return (
        input_grad[None],
        inner[None],
        new_first[None],
        new_second[None],
        new_anchor,
        new_momentum,
    )


def solution(mesh):
    in_specs = (
        P("group", "fsdp", None),
        P("group", "fsdp", None),
        P("group", "fsdp", None),
        P("group", "fsdp", None),
        P("group", "fsdp", None),
        P("fsdp", None),
        P("fsdp", None),
        P(),
    )
    out_specs = (
        P("group", "fsdp", None),
        P("group", "fsdp", None),
        P("group", "fsdp", None),
        P("group", "fsdp", None),
        P("fsdp", None),
        P("fsdp", None),
    )
    short = mesh.shape["fsdp"] == 8 and mesh.shape["group"] == 4
    return jax.shard_map(
        line if short else plain,
        mesh=mesh,
        in_specs=in_specs,
        out_specs=out_specs,
        check_vma=False,
    )
```

```python
import functools

import jax
import jax.numpy as jnp
from jax import lax
from jax.experimental import pallas as pl
from jax.experimental.pallas import tpu as pltpu
from jax.sharding import PartitionSpec as P

HEAD = 128
STEP = 100
CORR_ONE = 1.0 - 0.9**STEP
CORR_TWO = 1.0 - 0.95**STEP
PARTS = ((0, 256), (256, 256))
TILE = 256
BF16 = jnp.bfloat16
F32 = jnp.float32


def plain(
    activations,
    cotangent,
    inner_weights,
    first_moment,
    second_moment,
    anchor,
    outer_momentum,
    fragment,
):
    tokens_in = activations[0]
    upstream = cotangent[0]
    weights = inner_weights[0]
    low_weights = weights.astype(BF16)
    input_grad = lax.dot_general(
        upstream,
        lax.all_gather(low_weights, "fsdp", axis=0, tiled=True),
        (((1,), (1,)), ((), ())),
        preferred_element_type=F32,
    ).astype(BF16)
    gradient = lax.psum_scatter(
        lax.dot_general(tokens_in, upstream, (((0,), (0,)), ((), ())), preferred_element_type=F32),
        "fsdp",
        scatter_dimension=0,
        tiled=True,
    )
    new_first = 0.9 * first_moment[0] + 0.1 * gradient
    new_second = 0.95 * second_moment[0] + 0.05 * gradient * gradient
    update = new_first / CORR_ONE / (jnp.sqrt(new_second / CORR_TWO) + 1e-08) + 0.1 * weights
    stepped = weights - 0.1 * update
    offset = fragment[0] * HEAD
    local_cols = lax.dynamic_slice_in_dim(stepped, offset, HEAD, 1)
    anchor_cols = lax.dynamic_slice_in_dim(anchor, offset, HEAD, 1)
    moment_cols = lax.dynamic_slice_in_dim(outer_momentum, offset, HEAD, 1)
    summed = lax.psum((anchor_cols - local_cols).astype(BF16), "group").astype(F32)
    average = summed / lax.axis_size("group")
    moment_new = 0.9 * moment_cols + average
    anchor_next = anchor_cols - 0.7 * (average + 0.9 * moment_new)
    new_momentum = lax.dynamic_update_slice_in_dim(outer_momentum, moment_new, offset, 1)
    new_anchor = lax.dynamic_update_slice_in_dim(anchor, anchor_next, offset, 1)
    new_inner = lax.dynamic_update_slice_in_dim(stepped, anchor_next, offset, 1)
    return (
        input_grad[None],
        new_inner[None],
        new_first[None],
        new_second[None],
        new_anchor,
        new_momentum,
    )


def rows_by_columns(act, cot):
    return lax.dot_general(act, cot, (((0,), (0,)), ((), ())), preferred_element_type=F32)


def vmem(*shape, dtype=F32):
    return pltpu.VMEM(shape, dtype)


def hbm(*shape, dtype=F32):
    return jax.ShapeDtypeStruct(shape, dtype)


class Numbers:
    def __init__(self, ref):
        self.ref, self.read = ref, {}

    def __getitem__(self, k):
        if k not in self.read:
            self.read[k] = self.ref[0, k]
        return self.read[k]


class Held:
    def __init__(self, array):
        self.array = array


def call(body, scalars, ins, outs, scratch=(), aliases=None, after=(), us=1.0):
    arrays, specs = [], []
    for x in [*([] if scalars is None else [Held(scalars)]), *ins]:
        if isinstance(x, Held):
            arrays.append(pltpu.with_memory_space_constraint(x.array, pltpu.VMEM))
            specs.append(pl.BlockSpec(memory_space=pltpu.VMEM))
        else:
            arrays.append(pltpu.with_memory_space_constraint(x, pltpu.HBM))
            specs.append(pl.BlockSpec(memory_space=pltpu.HBM))
    first = len(arrays)
    arrays += [pltpu.with_memory_space_constraint(x, pltpu.VMEM) for x in after]
    specs += [pl.BlockSpec(memory_space=pltpu.VMEM)] * len(after)

    def inner(*refs):
        rest = refs[:first] + refs[first + len(after) :]
        body(*rest) if scalars is None else body(Numbers(rest[0]), *rest[1:])

    return pl.pallas_call(
        inner,
        in_specs=specs,
        out_specs=[
            pl.BlockSpec(memory_space=pl.ANY if isinstance(o, jax.ShapeDtypeStruct) else pltpu.VMEM)
            for o in outs
        ],
        out_shape=list(outs),
        scratch_shapes=list(scratch),
        input_output_aliases={1 + k: v for k, v in (aliases or {}).items()},
        cost_estimate=pl.CostEstimate(
            flops=0, bytes_accessed=int(us * 3.4e6), transcendentals=0
        ),
        compiler_params=pltpu.CompilerParams(vmem_limit_bytes=12 * 1024 * 1024),
    )(*arrays)


def columns_of(ref, block, width):
    return ref.at[:, pl.ds(pl.multiple_of(block * width, width), width)]


def start(src, dst, sem):
    copy = pltpu.make_async_copy(src, dst, sem)
    copy.start()
    return copy


def pieces(head):
    return (0, HEAD, head), (HEAD, HEAD, head ^ 1), (2 * HEAD, 2 * HEAD, 1 - head // 2)


def turned(at, s, src, dst, sems, base, first=0):
    return [
        start(
            columns_of(src, s[at["pieces"] + k], width),
            dst.at[:, pl.ds(column + first, width)],
            sems.at[base + k],
        )
        for k, (column, width, _) in enumerate(pieces(0))
    ]


def cast_body(offset, w, low, wide, sems):
    rows, part = low.shape
    chunks = 4
    step = rows // chunks
    copies = [
        start(
            w.at[pl.ds(i * step, step), pl.ds(offset, part)],
            wide.at[pl.ds(i * step, step)],
            sems.at[i],
        )
        for i in range(chunks)
    ]
    for i, copy in enumerate(copies):
        copy.wait()

        @pl.loop(0, step // 64)
        def _(n):
            here = pl.ds(pl.multiple_of(i * step + n * 64, 64), 64)
            low[here, :] = wide[here, :].astype(BF16)


def load_blocks(at, s, act, cot, act_s, cot_v, sems):
    heads = turned(at, s, cot, cot_v, sems, 0)
    rows = act_s.shape[2]
    blocks = [
        start(columns_of(act, 2 * d + s[at["core"]], rows), act_s.at[d], sems.at[len(heads) + d])
        for d in range(act_s.shape[0])
    ]
    return heads, blocks


def own_body(at, s, act, cot, anchor, moment, *rest):
    sums_ref, anchor_out, moment_out, act_s, cot_v, held, sems = rest
    chips, _, rows = act_s.shape
    heads, blocks = load_blocks(at, s, act, cot, act_s, cot_v, sems)
    base = len(heads) + chips
    loads = [start(src, held.at[k], sems.at[base + k]) for k, src in enumerate((anchor, moment))]
    stores = []
    for k, dst in enumerate((anchor_out, moment_out)):
        loads[k].wait()
        stores.append(start(held.at[k], dst, sems.at[base + 2 + k]))
    for copy in heads + blocks:
        copy.wait()

    @pl.loop(0, chips)
    def _(d):
        for i in range(rows // TILE):
            here = pl.ds(pl.multiple_of(d * rows + i * TILE, TILE), TILE)
            sums_ref[here, :] = rows_by_columns(
                act_s[d, :, i * TILE : (i + 1) * TILE], cot_v[...]
            )

    for copy in stores:
        copy.wait()


def sibling_body(at, s, before, act, cot, w, m, v, anchor, moment, *rest):
    sums_ref, w_v, m_v, v_v, anchor_v, moment_v, act_s, cot_v, sems = rest
    chips, _, rows = act_s.shape
    heads, blocks = load_blocks(at, s, act, cot, act_s, cot_v, sems)
    base = len(heads) + chips
    copies = []
    for src, dst in ((w, w_v), (m, m_v), (v, v_v)):
        copies += turned(at, s, src, dst, sems, base + len(copies))
    for src, dst in ((anchor, anchor_v), (moment, moment_v)):
        copies.append(
            start(columns_of(src, s[at["pieces"]], HEAD), dst, sems.at[base + len(copies)])
        )
    for copy in heads + blocks:
        copy.wait()

    @pl.loop(0, chips)
    def _(d):
        for i in range(rows // TILE):
            here = pl.ds(pl.multiple_of(d * rows + i * TILE, TILE), TILE)
            sums_ref[here, :] = before[here, :] + rows_by_columns(
                act_s[d, :, i * TILE : (i + 1) * TILE], cot_v[...]
            )

    for copy in copies:
        copy.wait()


def hop_body(at, step, offset, s, sums_ref, from_o, from_e, *rest):
    to_e, to_o, picked = rest[-3:]
    older = rest[0] if step == 3 else None
    rows, part = to_e.shape
    columns = slice(offset, offset + part)
    base = at["hop"] + 4 * (step - 1)
    size = 64

    def each(body):
        @pl.loop(0, rows // size)
        def _(i):
            body(pl.multiple_of(i * size, size))

    for mode, block, src, dst in (
        (s[base], s[base + 1], from_o, to_e),
        (s[base + 2], s[base + 3], from_e, to_o),
    ):
        first = pl.multiple_of(block * rows, rows)

        @pl.when(mode == 0)
        def _():
            def body(r):
                dst[pl.ds(r, size), :] = sums_ref[pl.ds(first + r, size), columns].astype(BF16)

            each(body)

        @pl.when(mode == 1)
        def _():
            def body(r):
                here = pl.ds(r, size)
                added = src[here, :].astype(F32) + sums_ref[pl.ds(first + r, size), columns]
                dst[here, :] = added.astype(BF16)

            each(body)

        @pl.when(mode == 2)
        def _():
            def body(r):
                dst[pl.ds(r, size), :] = src[pl.ds(r, size), :]

            each(body)

    def keep(src):
        def body(r):
            picked[pl.ds(r, size), :] = src[pl.ds(r, size), :]

        each(body)

    if step == 1:
        keep(from_e)
    else:

        @pl.when(s[at["middle"]] == 1)
        def _():
            keep(from_o if older is None else older)

        @pl.when(s[at["middle"]] == 0)
        def _():
            keep(from_e)


def grad_body(at, which, s, cot_own, cot_sib, *rest):
    theirs, out, token, stage, sems = rest[-5:]
    rows = stage.shape[1]
    copies = []
    if which > 0:
        copies.append(
            start(
                rest[len(PARTS)], columns_of(out, s[at["grad"] + 2 * which - 1], rows), sems.at[1]
            )
        )
    for cot, dst in ((cot_sib, theirs), (cot_own, stage)):
        for i in range(rows // TILE):
            here = slice(i * TILE, (i + 1) * TILE)
            total = None
            for (offset, part), block in zip(PARTS, rest):
                term = lax.dot_general(
                    cot[:, offset : offset + part],
                    block[here, :],
                    (((1,), (1,)), ((), ())),
                    preferred_element_type=F32,
                )
                total = term if total is None else total + term
            dst[:, here] = total.astype(BF16)
    copies.append(start(stage, columns_of(out, s[at["grad"] + 2 * which], rows), sems.at[0]))
    token[...] = jnp.zeros_like(token)
    for copy in copies:
        copy.wait()


def adam(at, offset, first_row, s, sums_ref, from_e, from_o, w, m, v, put, count, width, taken):
    columns = slice(offset, offset + width)
    size = 256
    base = pl.multiple_of(s[at["z"]] * from_e.shape[0], TILE)
    middle = s[at["middle"]] == 1

    @pl.loop(0, count // size)
    def _(i):
        r = pl.multiple_of(first_row + i * size, size)
        here = pl.ds(r, size)
        one = sums_ref[pl.ds(base + r, size), columns] + from_e[here, taken].astype(F32)
        both = one + from_o[here, taken].astype(F32)
        gradient = jnp.where(middle, both, one)
        first = 0.9 * m[here, columns] + 0.1 * gradient
        second = 0.95 * v[here, columns] + 0.05 * gradient * gradient
        below = second * lax.rsqrt(second) + 1e-08 * CORR_TWO**0.5
        moved = first * (0.1 * CORR_TWO**0.5 / CORR_ONE) / below
        stepped = (1.0 - 0.1 * 0.1) * w[here, columns] - moved
        put(r, stepped, first, second)


def head_body(at, s, sums_ref, from_e, from_o, w, m, v, anchor, upper, lower, first_v, second_v):
    rows = anchor.shape[0]
    for k, diff in enumerate((upper, lower)):
        top = k * rows // 2

        def put(r, stepped, first, second):
            here = pl.ds(r, stepped.shape[0])
            first_v[here, :] = first
            second_v[here, :] = second
            there = pl.ds(r - top, stepped.shape[0])
            diff[there, :] = (anchor[here, :] - stepped).astype(BF16)

        args = (from_e, from_o, w, m, v, put, rows // 2, HEAD, slice(0, HEAD))
        adam(at, 0, top, s, sums_ref, *args)


def rest_body(at, offset, part, within, s, sums_ref, from_e, from_o, w, m, v, *rest):
    stage, sems = rest[-2:]
    rows = from_e.shape[0]
    tiles = rows // TILE
    copies = []
    if within:
        first_v, second_v, theirs = rest[:3]
        *outs, grads, token = rest[4:-2]
        for k, src in enumerate((first_v, second_v)):
            there = columns_of(outs[1 + k], s[at["pieces"]], HEAD)
            copies.append(start(src, there, sems.at[k]))
        copies.append(start(theirs, columns_of(grads, s[at["grad"] + 7], rows), sems.at[2]))
        token[...] = jnp.zeros_like(token)
    else:
        tiles -= 1
        *outs, left = rest[3:-2]
    piece = next(k for k, (column, *_) in enumerate(pieces(0)) if column == offset)
    args = (from_e, from_o, w, m, v)
    taken = slice(within, within + part)

    def putter(refs, top):
        def put(r, *values):
            here = pl.ds(r - top, values[0].shape[0])
            for k, value in enumerate(values):
                refs[k, here, :] = value

        return put

    for tile in range(tiles):
        first = tile * TILE
        adam(at, offset, first, s, sums_ref, *args, putter(stage, 0), TILE, part, taken)
        there = pl.ds(first, TILE)
        for k, out in enumerate(outs):
            copies.append(
                start(
                    stage.at[k, there],
                    columns_of(out.at[there], s[at["pieces"] + piece], part),
                    sems.at[len(copies)],
                )
            )
    if not within:
        first = tiles * TILE
        adam(at, offset, first, s, sums_ref, *args, putter(left, first), TILE, part, taken)
    for copy in copies:
        copy.wait()


def mix(own, other, token):
    return (own.astype(F32) + other.astype(F32) + token[:1]).astype(BF16)


def outer_body(at, s, left, upper, upper_in, lower, lower_in, anchor, moment, *rest):
    inner, first, second, new_anchor, new_moment, stage, sems = rest[5:]
    rows = anchor.shape[0]
    _, count, part = left.shape
    there = pl.ds(rows - count, count)
    copies = []
    for k, out in enumerate((inner, first, second)):
        last = columns_of(out.at[there], s[at["pieces"] + 2], part)
        copies.append(start(left.at[k], last, sems.at[k]))
    half = rows // 2
    for n, (own, other) in enumerate(((upper, upper_in), (lower, lower_in))):
        there = pl.ds(n * half, half)
        average = (own[...].astype(F32) + other[...].astype(F32)) * 0.25
        momentum = 0.9 * moment[there, :] + average
        stage[0, there, :] = momentum
        stage[1, there, :] = anchor[there, :] - 0.7 * (average + 0.9 * momentum)
        for k, out in ((0, new_moment), (1, new_anchor), (1, inner)):
            target = columns_of(out.at[there], s[at["pieces"]], HEAD)
            copies.append(start(stage.at[k, there], target, sems.at[len(copies)]))
    for copy in copies:
        copy.wait()


def line(
    activations,
    cotangent,
    inner_weights,
    first_moment,
    second_moment,
    anchor,
    outer_momentum,
    fragment,
):
    act, cot, weights = activations[0], cotangent[0], inner_weights[0]
    moment, second = first_moment[0], second_moment[0]
    tokens, width = act.shape
    rows, columns = weights.shape
    chips = lax.axis_size("fsdp") // 2
    me = lax.axis_index("fsdp")
    z, core = me // 2, me % 2
    head = fragment[0]
    last = chips - 1
    middle = (z > 0) & (z < last)
    even = z % 2 == 0
    zd = last - z

    def cross(i):
        return i ^ 1 if i // 2 in (0, last) else (i + 2 if i // 2 % 2 else i - 2)

    e_perm = [(i, i ^ 2) for i in range(2 * chips)]
    o_perm = [(i, cross(i)) for i in range(2 * chips)]
    swap = [(i, i ^ 1) for i in range(2 * chips)]
    x_perm, y_perm = [(i, i ^ 1) for i in range(4)], [(i, i ^ 2) for i in range(4)]

    values, at = [], {}

    def name(key, *numbers):
        at[key] = len(values)
        values.extend(jnp.asarray(v, jnp.int32) for v in numbers)

    name("z", z)
    name("core", core)
    name("middle", middle)
    name("pieces", *[block for _, _, block in pieces(head)])
    name("grad", *[2 * (z ^ k) + c for k in range(chips) for c in (core, 1 - core)])
    hops = []
    for step in range(1, chips):
        up_mode = jnp.where(step <= z, 2, jnp.where(z == 0, 0, 1))
        down_mode = jnp.where(step <= zd, 2, jnp.where(zd == 0, 0, 1))
        up_to = jnp.clip(chips - step + z, 0, last)
        down_to = jnp.clip(step - 1 - zd, 0, last)
        hops += [
            jnp.where(even, up_mode, down_mode),
            jnp.where(even, up_to, down_to),
            jnp.where(middle, jnp.where(even, down_mode, up_mode), 2),
            jnp.where(even, down_to, up_to),
        ]
    name("hop", *hops)
    s = jnp.pad(jnp.stack(values), (0, 128 - len(values)))[None]

    def permute(x, perm, axis="fsdp"):
        return lax.ppermute(x, axis, perm)

    dma = pltpu.SemaphoreType.DMA
    from_e, from_o = [[]], [[]]
    act_sib, cot_sib = permute(act, swap), permute(cot, swap)
    low = []
    for (offset, part), after in zip(PARTS, ([], [cot_sib])):
        low += call(
            functools.partial(cast_body, offset),
            None,
            [weights],
            [vmem(rows, part, dtype=BF16)],
            [vmem(rows, part), dma((4,))],
            after=after,
            us=1.2,
        )
    for x in low:
        from_e[0].append(permute(x, e_perm))
        from_o[0].append(permute(x, o_perm))

    sums_shape = vmem(chips * rows, columns)
    cot_shape = vmem(tokens, columns, dtype=BF16)
    block_shape = vmem(chips, tokens, rows, dtype=BF16)
    sums_own, new_anchor, new_momentum = call(
        functools.partial(own_body, at),
        s,
        [act, Held(cot), anchor, outer_momentum],
        [sums_shape, hbm(rows, columns), hbm(rows, columns)],
        [block_shape, cot_shape, vmem(2, rows, columns), dma((chips + 7,))],
        after=low[-1:],
        us=5.0,
    )
    sums_both, w_v, m_v, v_v, anchor_v, moment_v = call(
        functools.partial(sibling_body, at),
        s,
        [Held(sums_own), act_sib, Held(cot_sib), weights, moment, second, anchor, outer_momentum],
        [sums_shape] + [vmem(rows, columns)] * 3 + [vmem(rows, HEAD)] * 2,
        [block_shape, cot_shape, dma((chips + 14,))],
        {0: 0},
        us=5.0,
    )

    def hop(step, j, after):
        offset, part = PARTS[j]
        ins = [Held(sums_both), Held(from_o[step - 1][j]), Held(from_e[step - 1][j])]
        if step == 3:
            ins += [Held(from_o[0][j])]
        return call(
            functools.partial(hop_body, at, step, offset),
            s,
            ins,
            [vmem(rows, part, dtype=BF16)] * 3,
            after=after,
        )

    def grad(which, before, own, after):
        ins = [Held(x) for x in [cot, cot_sib, *own]]
        aliases = {}
        if before is not None:
            theirs, buffer = before
            ins += [Held(theirs)]
            aliases = {len(ins): 1}
            ins += [buffer]
        theirs, buffer, token = call(
            functools.partial(grad_body, at, which),
            s,
            ins,
            [
                vmem(tokens, rows, dtype=BF16),
                hbm(tokens, width, dtype=BF16),
                vmem(8, 128),
            ],
            [vmem(tokens, rows, dtype=BF16), dma((2,))],
            aliases,
            after,
            us=2.1,
        )
        return (permute(theirs, swap), buffer), token

    grads, after, picked = None, (), low
    for step in range(1, chips):
        from_e.append([])
        from_o.append([])
        found = []
        for j in range(len(PARTS)):
            to_e, to_o, pick = hop(step, j, after)
            from_e[step].append(permute(to_e, e_perm))
            from_o[step].append(permute(to_o, o_perm))
            found.append(pick)
            after = ()
            if j == 0:
                grads, token = grad(step - 1, grads, picked, (to_e,))
                after = (token,)
        picked = found
    grads, token = grad(last, grads, picked, ())

    theirs, input_grad = grads
    half = vmem(rows // 2, HEAD, dtype=BF16)
    full = [hbm(rows, columns)] * 3

    def inputs(j):
        return [sums_both, from_e[last][j], from_o[last][j], w_v, m_v, v_v]

    upper, lower, first_v, second_v = call(
        functools.partial(head_body, at),
        s,
        [Held(x) for x in [*inputs(0), anchor_v]],
        [half, half, vmem(rows, HEAD), vmem(rows, HEAD)],
        after=(token,),
        us=1.0,
    )
    upper_in = permute(upper, x_perm, "group")
    lower_in = permute(lower, y_perm, "group")
    *state, input_grad, token = call(
        functools.partial(rest_body, at, HEAD, PARTS[0][1] - HEAD, HEAD),
        s,
        [Held(x) for x in [*inputs(0), first_v, second_v, theirs]] + [input_grad],
        full + [hbm(tokens, width, dtype=BF16), vmem(8, 128)],
        [vmem(3, rows, PARTS[0][1] - HEAD), dma((3 + 3 * rows // TILE,))],
        {9: 3},
        us=2.0,
    )
    upper, lower = mix(upper, upper_in, token), mix(lower, lower_in, token)
    upper_in = permute(upper, y_perm, "group")
    lower_in = permute(lower, x_perm, "group")
    offset, part = PARTS[1]
    *state, left = call(
        functools.partial(rest_body, at, offset, part, 0),
        s,
        [Held(x) for x in inputs(1)] + state,
        full + [vmem(3, TILE, part)],
        [vmem(3, rows, part), dma((3 * rows // TILE,))],
        {6: 0, 7: 1, 8: 2},
        after=(upper, lower),
        us=2.4,
    )
    held = [left, upper, upper_in, lower, lower_in, anchor_v, moment_v]
    inner, new_first, new_second, new_anchor, new_momentum = call(
        functools.partial(outer_body, at),
        s,
        [Held(x) for x in held] + [*state, new_anchor, new_momentum],
        [hbm(rows, columns)] * 5,
        [vmem(2, rows, HEAD), dma((9,))],
        {len(held) + k: k for k in range(5)},
        us=2.0,
    )
    return (
        input_grad[None],
        inner[None],
        new_first[None],
        new_second[None],
        new_anchor,
        new_momentum,
    )


def solution(mesh):
    in_specs = (
        P("group", "fsdp", None),
        P("group", "fsdp", None),
        P("group", "fsdp", None),
        P("group", "fsdp", None),
        P("group", "fsdp", None),
        P("fsdp", None),
        P("fsdp", None),
        P(),
    )
    out_specs = (
        P("group", "fsdp", None),
        P("group", "fsdp", None),
        P("group", "fsdp", None),
        P("group", "fsdp", None),
        P("fsdp", None),
        P("fsdp", None),
    )
    short = mesh.shape["fsdp"] == 8 and mesh.shape["group"] == 4
    return jax.shard_map(
        line if short else plain,
        mesh=mesh,
        in_specs=in_specs,
        out_specs=out_specs,
        check_vma=False,
    )
```
